256 devices in a mesh: scen: 32 (over y, x, core), fac: 8 (over z).
Axes of the slice: x: 4, y: 4, z: 8, core: 2. Of those that a mesh axis runs over, the one named last changes fastest.
Arguments:
- duals: bfloat16 [256, 4096, 128], P('scen', 'fac'), may hold values from -48 to 48
- tiles: bfloat16 [256, 1024, 4096], P('scen', 'fac'), may hold values from -0.5 to 0.5
- tile_rows: int32 [256, 1024], P('scen', 'fac'), may hold values from 0 to 7
- tile_cols: int32 [256, 1024], P('scen', 'fac'), may hold values from 0 to 39
- block_counts: int32 [256, 8], P('scen', 'fac'), may hold values from 32 to 128, as said below
- probabilities: float32 [256], P('scen'), may hold values from 0.001171875 to 0.01171875
- customer_map: int32 [64], replicated, may hold values from 0 to 7, as said below
- costs: float32 [20480, 128], P('fac'), may hold values from -6 to 6
Outputs:
- reduced: float32 [20480, 128], P('fac')
The draws below stay inside these ranges and needn't reach their ends.
Inputs may be any that keep to these rules, and one draw needn't show every extreme that they name: `customer_map`: in each aligned run of 8 customer blocks (the rows of one index of fac), every owner is named exactly 1 times. `block_counts`: every owner has some scenario with all 128 slots live.
All inputs are finite; a program needn't handle non-finite values.
Results may differ from the reference program's by a relative error of at most 0.0003.
Values may be sent and summed in bfloat16 or wider, within the bound.
A program may use at most 64 MiB of HBM per device.

```python
import math
import jax
import jax.numpy as jnp
from jax import lax

TILE = 64
P_SIZE = 128
CBD = 8
FBD = 40
NBD = 128
SCENARIOS = 256
CB = 64
PER_PAIR = 1
SLOTS = 1024
F = 20480


def draw_customer_map(key, part):
    key = jax.random.fold_in(key, 11)
    owners = CB // CBD
    key_list = jax.random.split(key, owners)
    orders = jax.vmap(lambda one_key: jax.random.permutation(one_key, CBD))(key_list)
    return (orders // PER_PAIR).reshape(CB).astype(jnp.int32)


def draw_block_counts(key, part):
    key = jax.random.fold_in(key, 12)
    owners = CB // CBD
    first_key, second_key, third_key = jax.random.split(key, 3)
    spread = jax.random.randint(first_key, (owners,), NBD // 8, NBD * 3 // 4 + 1)
    dropped = jax.random.randint(second_key, (SCENARIOS, owners), 0, spread[None, :] + 1)
    counted = NBD - dropped
    fullest = jax.random.randint(third_key, (owners,), 0, SCENARIOS)
    rows_index = jnp.arange(SCENARIOS, dtype=jnp.int32)[:, None]
    return jnp.where(rows_index == fullest[None, :], NBD, counted).astype(jnp.int32)


def touch_ends(values, own_key, least, high):
    extent = values.shape
    index_at = [jax.random.randint(jax.random.fold_in(own_key, axis), (), 0, extent[axis]) for axis in range(len(extent))]
    values = values.at[tuple(index_at)].set(least)
    longest = extent.index(max(extent))
    index_at[longest] = (index_at[longest] + 1) % extent[longest]
    return values.at[tuple(index_at)].set(high)


def shard_levels(rng, extent, cuts, low, high):
    loudness = 1.0
    for dim, blocks in cuts:
        heights = jax.random.uniform(jax.random.fold_in(jax.random.fold_in(rng, 6), dim), (blocks,), jnp.float32, low / len(cuts), high / len(cuts))
        loudness = loudness * jnp.repeat(jnp.exp(heights), extent[dim] // blocks).reshape((-1,) + (1,) * (len(extent) - 1 - dim))
    return loudness


def centred(rng, dims, scale, most, pieces=(), held_as=jnp.bfloat16):
    loudness = shard_levels(rng, dims, pieces, -0.22, 0.18) if pieces else 1.0
    drawn = jax.random.normal(rng, dims, jnp.float32) * scale * loudness
    return jnp.minimum(jnp.maximum(drawn, -most), most).astype(held_as)


def setup_inputs(seed: int = 0) -> dict:
    seeds = jax.random.split(jax.random.key(seed), 9)
    duals = centred(seeds[0], (SCENARIOS, CB * TILE, P_SIZE), (SCENARIOS ** 0.5 / 2), 48.0, ((0, 32), (1, 8)))
    tiles = centred(seeds[1], (SCENARIOS, SLOTS, TILE * TILE), (2 * TILE) ** -0.5, 0.5, ((0, 32), (1, 8)))
    tile_rows = touch_ends(jax.random.randint(seeds[2], (SCENARIOS, SLOTS), 0, CBD), jax.random.fold_in(seeds[2], 1), 0, CBD - 1).astype(jnp.int32)
    tile_cols = touch_ends(jax.random.randint(seeds[3], (SCENARIOS, SLOTS), 0, FBD), jax.random.fold_in(seeds[3], 1), 0, FBD - 1).astype(jnp.int32)
    block_counts = draw_block_counts(jax.random.fold_in(seeds[8], 71), 0)
    probabilities = jnp.clip(jnp.exp(math.log(0.01171875) - 2.3025851 * jax.random.uniform(seeds[5], (SCENARIOS,), jnp.float32) ** shard_levels(seeds[5], (SCENARIOS,), ((0, 32),), -0.2, 0.2)), 0.001171875, 0.01171875)
    customer_map = draw_customer_map(jax.random.fold_in(seeds[8], 71), 0)
    costs = centred(seeds[7], (F, P_SIZE), 1.0, 6.0, ((0, 8),), jnp.float32)
    return {"duals": duals, "tiles": tiles, "tile_rows": tile_rows, "tile_cols": tile_cols, "block_counts": block_counts, "probabilities": probabilities, "customer_map": customer_map, "costs": costs}


def reference(duals, tiles, tile_rows, tile_cols, block_counts, probabilities, customer_map, costs):
    blocks_all = customer_map.shape[0]
    owners = blocks_all // CBD
    periods = duals.shape[2]
    sort_keys = customer_map.astype(jnp.int32) * blocks_all + jnp.arange(blocks_all, dtype=jnp.int32)
    ordering = jnp.argsort(sort_keys).astype(jnp.int32)
    slot_owner = jnp.arange(owners * NBD, dtype=jnp.int32) // NBD
    position = jnp.arange(owners * NBD, dtype=jnp.int32) % NBD
    dual_blocks = duals.reshape(duals.shape[0], blocks_all, TILE, periods)

    def scenario_sum(running, inputs):
        tile_set, row_set, col_set, live_count, weight, block_duals = inputs
        square_set = tile_set.reshape(tile_set.shape[0], TILE, TILE)
        global_rows = ordering[slot_owner * CBD + row_set.astype(jnp.int32)]
        picked = block_duals[global_rows].astype(jnp.float32)
        products = jnp.einsum("tji,tip->tjp", square_set.astype(jnp.float32), picked, precision=lax.Precision.HIGHEST)
        scaled = jnp.where(position < live_count[slot_owner], weight, jnp.float32(0.0))
        target = slot_owner * FBD + col_set.astype(jnp.int32)
        running = running + jax.ops.segment_sum(products * scaled[:, None, None], target, num_segments=owners * FBD)
        return running, None

    initial = jnp.zeros((owners * FBD, TILE, periods), jnp.float32)
    gradient = lax.scan(scenario_sum, initial, (tiles, tile_rows, tile_cols, block_counts, probabilities, dual_blocks))[0]
    return costs - gradient.reshape(owners * FBD * TILE, periods)
```

```python
import functools

import jax
import jax.numpy as jnp
from jax import lax
from jax.experimental import pallas as pl
from jax.experimental.pallas import tpu as pltpu
from jax.sharding import PartitionSpec as P

TILE = 64
FBD = 40
SLOTS = 128
LANES = 128
PAIRS = TILE // 2
WIDE = 16
HALF = PAIRS * FBD
MESH = pl.DeviceIdType.MESH


def exchange_kernel(
    ny,
    nx,
    nz,
    scen,
    duals_hbm,
    tiles_hbm,
    rows_ref,
    cols_ref,
    counts_ref,
    prob_ref,
    map_ref,
    out_hbm,
    duals_v,
    tiles_v,
    stage,
    land,
    selector,
    high,
    low,
    weights,
    acc,
    core_in,
    x_in,
    y_in,
    x_sum,
    y_sum,
    x_in2,
    y_in2,
    full,
    duals_sem,
    tiles_sem,
    z_send,
    z_recv,
    c_send,
    c_recv,
    r_send,
    r_recv,
    q_send,
    q_recv,
    g_send,
    g_recv,
    h_send,
    h_recv,
    f_send,
    f_recv,
    out_sem,
):
    sc = lax.axis_index("scen")
    me = lax.axis_index("fac")
    core = lax.rem(sc, 2)
    xx = lax.rem(lax.div(sc, 2), nx)
    yy = lax.div(sc, 2 * nx)

    def at(y, x, c):
        return (lax.rem(y, ny) * nx + lax.rem(x, nx)) * 2 + c

    duals_copy = pltpu.make_async_copy(duals_hbm, duals_v, duals_sem)
    duals_copy.start()

    barrier = pltpu.get_barrier_semaphore()
    peers = 0
    for d in range(1, nz):
        pl.semaphore_signal(barrier, inc=1, device_id=(sc, lax.rem(me + d, nz)), device_id_type=MESH)
        peers += 1
    for d in range(1, nx):
        pl.semaphore_signal(barrier, inc=1, device_id=(at(yy, xx + d, core), me), device_id_type=MESH)
        peers += 1
    for d in range(1, ny):
        pl.semaphore_signal(barrier, inc=1, device_id=(at(yy + d, xx, core), me), device_id_type=MESH)
        peers += 1
    pl.semaphore_signal(barrier, inc=1, device_id=(at(yy, xx, 1 - core), me), device_id_type=MESH)
    peers += 1

    def tiles_copy(s):
        return pltpu.make_async_copy(tiles_hbm.at[s], tiles_v.at[s], tiles_sem.at[s])

    @pl.loop(0, scen)
    def _(s):
        tiles_copy(s).start()

    owners = [map_ref[me * nz + k] for k in range(nz)]
    keep = [[jnp.where(owner == o, 1.0, 0.0) for owner in owners] for o in range(nz)]

    weights[...] = jnp.zeros_like(weights)
    acc[...] = jnp.zeros_like(acc)
    duals_copy.wait()

    @pl.loop(0, scen)
    def _(s):
        blocks = [duals_v[s, k * TILE : (k + 1) * TILE, :].astype(jnp.float32) for k in range(nz)]
        for o in range(nz):
            block = blocks[0] * keep[o][0]
            for k in range(1, nz):
                block = block + blocks[k] * keep[o][k]
            stage[s, o] = block.astype(jnp.bfloat16)

    pl.semaphore_wait(barrier, peers)

    def z_copy(s, d):
        to = lax.rem(me + d, nz)
        return pltpu.make_async_remote_copy(
            src_ref=stage.at[s, to],
            dst_ref=land.at[s, me],
            send_sem=z_send.at[s, d],
            recv_sem=z_recv.at[s, d],
            device_id=(sc, to),
            device_id_type=MESH,
        )

    def z_arrival(s, d):
        source = lax.rem(me + nz - d, nz)
        return pltpu.make_async_remote_copy(
            src_ref=stage.at[s, source],
            dst_ref=land.at[s, source],
            send_sem=z_send.at[s, d],
            recv_sem=z_recv.at[s, d],
            device_id=(sc, source),
            device_id_type=MESH,
        )

    order = sorted(range(1, nz), key=lambda d: -min(d, nz - d))

    @pl.loop(0, scen)
    def _(s):
        for d in order:
            z_copy(s, d).start()
        land[s, me] = stage[s, me]

    position = lax.broadcasted_iota(jnp.int32, rows_ref.shape, 1)
    cells = jnp.where(position < counts_ref[...], rows_ref[...] * FBD + cols_ref[...], -1)
    cell_ids = lax.broadcasted_iota(jnp.int32, (nz * FBD, SLOTS), 0)
    row_ids = lax.broadcasted_iota(jnp.int32, rows_ref.shape, 0)

    @pl.loop(0, scen)
    def _(s):
        mine = jnp.sum(jnp.where(row_ids == s, cells, 0), axis=0, keepdims=True)
        selector[...] = jnp.where(cell_ids == mine, 1.0, 0.0).astype(jnp.bfloat16)
        tiles_copy(s).wait()

        for n in range(WIDE):
            block = tiles_v[s, :, n * 256 : (n + 1) * 256]
            dense = jnp.dot(selector[...], block, preferred_element_type=jnp.float32)
            for r in range(nz):
                part = dense[r * FBD : (r + 1) * FBD]
                both = jnp.concatenate([part[:, :LANES], part[:, LANES:]], axis=0)
                upper = both.astype(jnp.bfloat16)
                lower = (both - upper.astype(jnp.float32)).astype(jnp.bfloat16)
                high[n * 80 : (n + 1) * 80, r * LANES : (r + 1) * LANES] = upper
                low[n * 80 : (n + 1) * 80, r * LANES : (r + 1) * LANES] = lower

        for d in range(1, nz):
            z_arrival(s, d).wait_recv()
        for r in range(nz):
            block = land[s, r]
            weights[r * LANES : r * LANES + TILE, :LANES] = block
            weights[r * LANES + TILE : (r + 1) * LANES, LANES:] = block

        scale = prob_ref[s]
        for n in range(4):
            rows = slice(n * 320, (n + 1) * 320)
            value = jnp.dot(high[rows], weights[...], preferred_element_type=jnp.float32)
            value = value + jnp.dot(low[rows], weights[...], preferred_element_type=jnp.float32)
            value = value * scale
            acc[n * 320 : (n + 1) * 320, :] += value[:, :LANES]
            acc[HALF + n * 320 : HALF + (n + 1) * 320, :] += value[:, LANES:]

    @pl.loop(0, scen)
    def _(s):
        for d in range(1, nz):
            z_copy(s, d).wait_send()

    part = HALF // 2
    mine = core * HALF
    other = (1 - core) * HALF
    sibling = (at(yy, xx, 1 - core), me)

    def core_copy(k):
        return pltpu.make_async_remote_copy(
            src_ref=acc.at[pl.ds(other + k * part, part)],
            dst_ref=core_in.at[pl.ds(k * part, part)],
            send_sem=c_send.at[k],
            recv_sem=c_recv.at[k],
            device_id=sibling,
            device_id_type=MESH,
        )

    for k in range(2):
        core_copy(k).start()

    first = (nx, ny)
    second = (ny, nx)
    spot = (xx, yy)
    spot2 = (yy, xx)
    inbox = (x_in, y_in)
    inbox2 = (x_in2, y_in2)
    sums = (x_sum, y_sum)

    def peer(k, d, n):
        along_x = (k == 0) == (n == 0)
        return (at(yy, xx + d, core) if along_x else at(yy + d, xx, core), me)

    def size1(k):
        return part // first[k]

    def size2(k):
        return size1(k) // second[k]

    def r_copy(k, d):
        to = lax.rem(spot[k] + d, first[k])
        return pltpu.make_async_remote_copy(
            src_ref=acc.at[pl.ds(mine + k * part + to * size1(k), size1(k))],
            dst_ref=inbox[k].at[d - 1],
            send_sem=r_send.at[k, d],
            recv_sem=r_recv.at[k, d],
            device_id=peer(k, d, 0),
            device_id_type=MESH,
        )

    def q_copy(k, d):
        to = lax.rem(spot2[k] + d, second[k])
        return pltpu.make_async_remote_copy(
            src_ref=sums[k].at[pl.ds(to * size2(k), size2(k))],
            dst_ref=inbox2[k].at[d - 1],
            send_sem=q_send.at[k, d],
            recv_sem=q_recv.at[k, d],
            device_id=peer(k, d, 1),
            device_id_type=MESH,
        )

    def big(k, x):
        return mine + k * part + x * size1(k)

    def small(k, y):
        return big(k, spot[k]) + y * size2(k)

    def g_copy(k, d, y):
        rows = full.at[pl.ds(small(k, y), size2(k))]
        return pltpu.make_async_remote_copy(
            src_ref=rows,
            dst_ref=rows,
            send_sem=g_send.at[k, d],
            recv_sem=g_recv.at[k, d],
            device_id=peer(k, d, 1),
            device_id_type=MESH,
        )

    def h_copy(k, d, x):
        rows = full.at[pl.ds(big(k, x), size1(k))]
        return pltpu.make_async_remote_copy(
            src_ref=rows,
            dst_ref=rows,
            send_sem=h_send.at[k, d],
            recv_sem=h_recv.at[k, d],
            device_id=peer(k, d, 0),
            device_id_type=MESH,
        )

    def f_copy(k, d, base):
        x = lax.rem(spot[k] + first[k] - d, first[k])
        rows = full.at[pl.ds(base + k * part + x * size1(k), size1(k))]
        return pltpu.make_async_remote_copy(
            src_ref=rows,
            dst_ref=rows,
            send_sem=f_send.at[k, d],
            recv_sem=f_recv.at[k, d],
            device_id=sibling,
            device_id_type=MESH,
        )

    for k in range(2):
        core_copy(k).wait_recv()
        here = pl.ds(mine + k * part, part)
        acc[here, :] += core_in[k * part : (k + 1) * part, :]
        for d in range(1, first[k]):
            r_copy(k, d).start()
    for k in range(2):
        total = acc[pl.ds(big(k, spot[k]), size1(k)), :]
        for d in range(1, first[k]):
            r_copy(k, d).wait_recv()
            total = total + inbox[k][d - 1]
        sums[k][...] = total
        for d in range(1, second[k]):
            q_copy(k, d).start()
    for k in range(2):
        total = sums[k][pl.ds(spot2[k] * size2(k), size2(k)), :]
        for d in range(1, second[k]):
            q_copy(k, d).wait_recv()
            total = total + inbox2[k][d - 1]
        full[pl.ds(small(k, spot2[k]), size2(k)), :] = total
        for d in range(1, second[k]):
            g_copy(k, d, spot2[k]).start()
    for k in range(2):
        for d in range(1, second[k]):
            g_copy(k, d, lax.rem(spot2[k] + second[k] - d, second[k])).wait_recv()
        for d in range(1, first[k]):
            h_copy(k, d, spot[k]).start()
        f_copy(k, 0, mine).start()
    for d in range(1, max(first)):
        for k in range(2):
            if d < first[k]:
                h_copy(k, d, lax.rem(spot[k] + first[k] - d, first[k])).wait_recv()
                f_copy(k, d, mine).start()
    for k in range(2):
        for d in range(first[k]):
            f_copy(k, d, other).wait_recv()
    out_copy = pltpu.make_async_copy(full, out_hbm, out_sem)
    out_copy.start()
    for k in range(2):
        core_copy(k).wait_send()
        for d in range(1, first[k]):
            r_copy(k, d).wait_send()
            h_copy(k, d, spot[k]).wait_send()
        for d in range(1, second[k]):
            q_copy(k, d).wait_send()
            g_copy(k, d, spot2[k]).wait_send()
        for d in range(first[k]):
            f_copy(k, d, mine).wait_send()
    out_copy.wait()


def finish_kernel(costs_ref, gradient_ref, out_ref):
    for j in range(TILE):
        at = (j % 2) * HALF + (j // 2) * FBD
        rows = pl.ds(j, FBD, stride=TILE)
        out_ref[rows, :] = costs_ref[rows, :] - gradient_ref[at : at + FBD, :]


def local(ny, nx, nz, duals, tiles, tile_rows, tile_cols, block_counts, probabilities, customer_map, costs):
    scen = duals.shape[0]
    bf16, f32 = jnp.bfloat16, jnp.float32
    part = HALF // 2
    vmem = pl.BlockSpec(memory_space=pltpu.VMEM)
    smem = pl.BlockSpec(memory_space=pltpu.SMEM)
    far = pl.BlockSpec(memory_space=pl.ANY)
    dma = pltpu.SemaphoreType.DMA
    most = max(nx, ny)
    gradient = pl.pallas_call(
        functools.partial(exchange_kernel, ny, nx, nz, scen),
        out_shape=jax.ShapeDtypeStruct((2 * HALF, LANES), f32),
        in_specs=[far, far, vmem, vmem, vmem, smem, smem],
        out_specs=far,
        scratch_shapes=[
            pltpu.VMEM(duals.shape, bf16),
            pltpu.VMEM(tiles.shape, bf16),
            pltpu.VMEM((scen, nz, TILE, LANES), bf16),
            pltpu.VMEM((scen, nz, TILE, LANES), bf16),
            pltpu.VMEM((nz * FBD, SLOTS), bf16),
            pltpu.VMEM((HALF, nz * LANES), bf16),
            pltpu.VMEM((HALF, nz * LANES), bf16),
            pltpu.VMEM((nz * LANES, 2 * LANES), bf16),
            pltpu.VMEM((2 * HALF, LANES), f32),
            pltpu.VMEM((HALF, LANES), f32),
            pltpu.VMEM((nx - 1, part // nx, LANES), f32),
            pltpu.VMEM((ny - 1, part // ny, LANES), f32),
            pltpu.VMEM((part // nx, LANES), f32),
            pltpu.VMEM((part // ny, LANES), f32),
            pltpu.VMEM((ny - 1, part // nx // ny, LANES), f32),
            pltpu.VMEM((nx - 1, part // nx // ny, LANES), f32),
            pltpu.VMEM((2 * HALF, LANES), f32),
            dma,
            dma((scen,)),
            dma((scen, nz)),
            dma((scen, nz)),
            dma((2,)),
            dma((2,)),
            dma((2, most)),
            dma((2, most)),
            dma((2, most)),
            dma((2, most)),
            dma((2, most)),
            dma((2, most)),
            dma((2, most)),
            dma((2, most)),
            dma((2, most)),
            dma((2, most)),
            dma,
        ],
        compiler_params=pltpu.CompilerParams(
            collective_id=0, has_side_effects=True, vmem_limit_bytes=48 * 2**20
        ),
        name="exchange",
    )(duals, tiles, tile_rows, tile_cols, block_counts, probabilities, customer_map)
    return pl.pallas_call(
        finish_kernel,
        out_shape=jax.ShapeDtypeStruct(costs.shape, f32),
        in_specs=[vmem, vmem],
        out_specs=vmem,
        compiler_params=pltpu.CompilerParams(vmem_limit_bytes=32 * 2**20),
        name="finish",
    )(costs, gradient)


def solution(mesh):
    nz = mesh.shape["fac"]
    chips = mesh.shape["scen"] // 2
    side = 1
    while side * side < chips:
        side += 1
    in_specs = (
        P("scen", "fac", None),
        P("scen", "fac", None),
        P("scen", "fac"),
        P("scen", "fac"),
        P("scen", "fac"),
        P("scen"),
        P(),
        P("fac", None),
    )
    out_specs = P("fac", None)
    return jax.shard_map(
        functools.partial(local, side, side, nz),
        mesh=mesh,
        in_specs=in_specs,
        out_specs=out_specs,
        check_vma=False,
    )
```

```python
import functools

import jax
import jax.numpy as jnp
from jax import lax
from jax.experimental import pallas as pl
from jax.experimental.pallas import tpu as pltpu
from jax.sharding import PartitionSpec as P

TILE = 64
FBD = 40
SLOTS = 128
LANES = 128
PAIRS = TILE // 2
WIDE = 16
DEEP = 5
CHUNKS = ((0, 40),)
MESH = pl.DeviceIdType.MESH


def exchange_kernel(
    ny,
    nx,
    nz,
    scen,
    duals_hbm,
    tiles_hbm,
    rows_hbm,
    cols_hbm,
    counts_hbm,
    prob_hbm,
    map_hbm,
    out,
    rows_ref,
    cols_ref,
    counts_ref,
    prob_ref,
    map_ref,
    duals_v,
    tiles_v,
    stage,
    land,
    selector,
    high,
    low,
    weights,
    acc,
    core_in,
    x_in,
    y_in,
    x_sum,
    y_sum,
    x_in2,
    y_in2,
    x_last,
    y_last,
    small_sem,
    duals_sem,
    tiles_sem,
    z_send,
    z_recv,
    c_send,
    c_recv,
    r_send,
    r_recv,
    q_send,
    q_recv,
    g_send,
    g_recv,
    h_send,
    h_recv,
    f_send,
    f_recv,
    own_sem,
):
    sc = lax.axis_index("scen")
    me = lax.axis_index("fac")
    core = lax.rem(sc, 2)
    xx = lax.rem(lax.div(sc, 2), nx)
    yy = lax.div(sc, 2 * nx)

    def at(y, x, c):
        return (lax.rem(y, ny) * nx + lax.rem(x, nx)) * 2 + c

    sibling = (at(yy, xx, 1 - core), me)

    barrier = pltpu.get_barrier_semaphore()
    peers = [(sc, lax.rem(me + d, nz)) for d in range(1, nz)]
    peers += [(at(yy, xx + d, core), me) for d in range(1, nx)]
    peers += [(at(yy + d, xx, core), me) for d in range(1, ny)]
    peers.append(sibling)
    for one in peers:
        pl.semaphore_signal(barrier, inc=1, device_id=one, device_id_type=MESH)

    duals_copy = pltpu.make_async_copy(duals_hbm, duals_v, duals_sem)
    pairs = ((map_hbm, map_ref), (rows_hbm, rows_ref), (cols_hbm, cols_ref), (counts_hbm, counts_ref), (prob_hbm, prob_ref))
    smalls = [pltpu.make_async_copy(src, dst, small_sem.at[n]) for n, (src, dst) in enumerate(pairs)]
    smalls[0].start()
    duals_copy.start()
    for one in smalls[1:]:
        one.start()

    def tiles_copy(s):
        return pltpu.make_async_copy(tiles_hbm.at[s], tiles_v.at[s], tiles_sem.at[s])

    @pl.loop(0, scen)
    def _(s):
        tiles_copy(s).start()

    weights[...] = jnp.zeros_like(weights)
    acc[...] = jnp.zeros_like(acc)
    for one in smalls:
        one.wait()

    owners = [map_ref[me * nz + k] for k in range(nz)]
    keep = [[jnp.where(owner == o, 1.0, 0.0) for owner in owners] for o in range(nz)]
    duals_copy.wait()

    @pl.loop(0, scen)
    def _(s):
        blocks = [duals_v[s, k * TILE : (k + 1) * TILE, :].astype(jnp.float32) for k in range(nz)]
        for o in range(nz):
            block = blocks[0] * keep[o][0]
            for k in range(1, nz):
                block = block + blocks[k] * keep[o][k]
            stage[s, o] = block.astype(jnp.bfloat16)

    def densify(s):
        slot = lax.rem(s, DEEP)
        position = lax.broadcasted_iota(jnp.int32, (1, SLOTS), 1)
        cells = rows_ref[pl.ds(s, 1), :] * FBD + cols_ref[pl.ds(s, 1), :]
        cells = jnp.where(position < counts_ref[s], cells, -1)
        cell_ids = lax.broadcasted_iota(jnp.int32, (nz * FBD, SLOTS), 0)
        selector[...] = jnp.where(cell_ids == cells, 1.0, 0.0).astype(jnp.bfloat16)
        tiles_copy(s).wait()
        for n in range(WIDE):
            block = tiles_v[s, :, n * 256 : (n + 1) * 256]
            dense = jnp.dot(selector[...], block, preferred_element_type=jnp.float32)
            for r in range(nz):
                part = dense[r * FBD : (r + 1) * FBD]
                both = jnp.concatenate([part[:, :LANES], part[:, LANES:]], axis=0)
                upper = both.astype(jnp.bfloat16)
                lower = (both - upper.astype(jnp.float32)).astype(jnp.bfloat16)
                high[slot, n * 80 : (n + 1) * 80, r * LANES : (r + 1) * LANES] = upper
                low[slot, n * 80 : (n + 1) * 80, r * LANES : (r + 1) * LANES] = lower

    densify(0)
    pl.semaphore_wait(barrier, len(peers))

    def z_copy(s, d):
        to = lax.rem(me + d, nz)
        return pltpu.make_async_remote_copy(
            src_ref=stage.at[s, to],
            dst_ref=land.at[s, me],
            send_sem=z_send.at[s, d],
            recv_sem=z_recv.at[s, d],
            device_id=(sc, to),
            device_id_type=MESH,
        )

    def z_arrival(s, d):
        source = lax.rem(me + nz - d, nz)
        return pltpu.make_async_remote_copy(
            src_ref=stage.at[s, source],
            dst_ref=land.at[s, source],
            send_sem=z_send.at[s, d],
            recv_sem=z_recv.at[s, d],
            device_id=(sc, source),
            device_id_type=MESH,
        )

    order = sorted(range(1, nz), key=lambda d: -min(d, nz - d))

    @pl.loop(0, scen)
    def _(s):
        for d in order:
            z_copy(s, d).start()
        land[s, me] = stage[s, me]

    @pl.loop(1, min(DEEP, scen))
    def _(s):
        densify(s)

    first = (nx, ny)
    second = (ny, nx)
    spot = (xx, yy)
    spot2 = (yy, xx)
    inbox = (x_in, y_in)
    inbox2 = (x_in2, y_in2)
    sums = (x_sum, y_sum)
    last = (x_last, y_last)
    part = PAIRS // 2
    size1 = [part // n for n in first]
    size2 = [part // (ny * nx)] * 2
    mine = core * PAIRS
    other = (1 - core) * PAIRS

    def columns(h):
        return pl.ds(CHUNKS[h][0], CHUNKS[h][1])

    def core_copy(k, h):
        return pltpu.make_async_remote_copy(
            src_ref=acc.at[pl.ds(other + k * part, part), columns(h)],
            dst_ref=core_in.at[pl.ds(k * part, part), columns(h)],
            send_sem=c_send.at[k, h],
            recv_sem=c_recv.at[k, h],
            device_id=sibling,
            device_id_type=MESH,
        )

    @pl.loop(0, scen)
    def _(s):
        slot = lax.rem(s, DEEP)
        for d in range(1, nz):
            z_arrival(s, d).wait_recv()
        for r in range(nz):
            block = land[s, r]
            weights[r * LANES : r * LANES + TILE, :LANES] = block
            weights[r * LANES + TILE : (r + 1) * LANES, LANES:] = block

        scale = prob_ref[s]
        for n in range(4):
            rows = slice(n * 320, (n + 1) * 320)
            value = jnp.dot(high[slot, rows], weights[...], preferred_element_type=jnp.float32)
            value = value + jnp.dot(low[slot, rows], weights[...], preferred_element_type=jnp.float32)
            value = value * scale
            acc[n * 8 : (n + 1) * 8] += value[:, :LANES].reshape(8, FBD, LANES)
            acc[PAIRS + n * 8 : PAIRS + (n + 1) * 8] += value[:, LANES:].reshape(8, FBD, LANES)
            if n % 2:

                @pl.when(s == scen - 1)
                def _():
                    for h in range(len(CHUNKS)):
                        core_copy(n // 2, h).start()

        @pl.when(s < scen - DEEP)
        def _():
            densify(s + DEEP)

    def peer(k, d, n):
        along_x = (k == 0) == (n == 0)
        return (at(yy, xx + d, core) if along_x else at(yy + d, xx, core), me)

    def big(k, x):
        return mine + k * part + x * size1[k]

    def small(k, y):
        return big(k, spot[k]) + y * size2[k]

    def r_copy(k, h, d):
        to = lax.rem(spot[k] + d, first[k])
        return pltpu.make_async_remote_copy(
            src_ref=acc.at[pl.ds(big(k, to), size1[k]), columns(h)],
            dst_ref=inbox[k].at[d - 1, :, columns(h)],
            send_sem=r_send.at[k, h, d],
            recv_sem=r_recv.at[k, h, d],
            device_id=peer(k, d, 0),
            device_id_type=MESH,
        )

    def q_copy(k, h, d):
        to = lax.rem(spot2[k] + d, second[k])
        return pltpu.make_async_remote_copy(
            src_ref=sums[k].at[pl.ds(to * size2[k], size2[k]), columns(h)],
            dst_ref=inbox2[k].at[d - 1, :, columns(h)],
            send_sem=q_send.at[k, h, d],
            recv_sem=q_recv.at[k, h, d],
            device_id=peer(k, d, 1),
            device_id_type=MESH,
        )

    def g_copy(k, h, d, y):
        return pltpu.make_async_remote_copy(
            src_ref=last[k].at[:, columns(h)],
            dst_ref=out.at[pl.ds(small(k, y), size2[k]), columns(h)],
            send_sem=g_send.at[k, h, d],
            recv_sem=g_recv.at[k, h, d],
            device_id=peer(k, d, 1),
            device_id_type=MESH,
        )

    def own_copy(k, h):
        return pltpu.make_async_copy(
            last[k].at[:, columns(h)],
            out.at[pl.ds(small(k, spot2[k]), size2[k]), columns(h)],
            own_sem.at[k, h],
        )

    def h_copy(k, h, d, x):
        block = out.at[pl.ds(big(k, x), size1[k]), columns(h)]
        return pltpu.make_async_remote_copy(
            src_ref=block,
            dst_ref=block,
            send_sem=h_send.at[k, h, d],
            recv_sem=h_recv.at[k, h, d],
            device_id=peer(k, d, 0),
            device_id_type=MESH,
        )

    def f_copy(k, h, d, base):
        x = lax.rem(spot[k] + first[k] - d, first[k])
        block = out.at[pl.ds(base + k * part + x * size1[k], size1[k]), columns(h)]
        return pltpu.make_async_remote_copy(
            src_ref=block,
            dst_ref=block,
            send_sem=f_send.at[k, h, d],
            recv_sem=f_recv.at[k, h, d],
            device_id=sibling,
            device_id_type=MESH,
        )

    pieces = [(k, h) for h in range(len(CHUNKS)) for k in range(2)]
    for k, h in pieces:
        core_copy(k, h).wait_recv()
        here = pl.ds(mine + k * part, part)
        acc[here, columns(h)] += core_in[k * part : (k + 1) * part, columns(h)]
        for d in range(1, first[k]):
            r_copy(k, h, d).start()
    for k, h in pieces:
        total = acc[pl.ds(big(k, spot[k]), size1[k]), columns(h)]
        for d in range(1, first[k]):
            r_copy(k, h, d).wait_recv()
            total = total + inbox[k][d - 1, :, columns(h)]
        sums[k][:, columns(h)] = total
        for d in range(1, second[k]):
            q_copy(k, h, d).start()
    for k, h in pieces:
        total = sums[k][pl.ds(spot2[k] * size2[k], size2[k]), columns(h)]
        for d in range(1, second[k]):
            q_copy(k, h, d).wait_recv()
            total = total + inbox2[k][d - 1, :, columns(h)]
        last[k][:, columns(h)] = total
        for d in range(1, second[k]):
            g_copy(k, h, d, spot2[k]).start()
        own_copy(k, h).start()
    for k, h in pieces:
        own_copy(k, h).wait()
        for d in range(1, second[k]):
            g_copy(k, h, d, lax.rem(spot2[k] + second[k] - d, second[k])).wait_recv()
        for d in range(1, first[k]):
            h_copy(k, h, d, spot[k]).start()
        f_copy(k, h, 0, mine).start()
    for k, h in pieces:
        for d in range(1, first[k]):
            h_copy(k, h, d, lax.rem(spot[k] + first[k] - d, first[k])).wait_recv()
            f_copy(k, h, d, mine).start()

    @pl.loop(0, scen)
    def _(s):
        for d in range(1, nz):
            z_copy(s, d).wait_send()

    for k, h in pieces:
        core_copy(k, h).wait_send()
        for d in range(1, first[k]):
            r_copy(k, h, d).wait_send()
            h_copy(k, h, d, spot[k]).wait_send()
        for d in range(1, second[k]):
            q_copy(k, h, d).wait_send()
            g_copy(k, h, d, spot2[k]).wait_send()
        for d in range(first[k]):
            f_copy(k, h, d, mine).wait_send()
    for k, h in pieces:
        for d in range(first[k]):
            f_copy(k, h, d, other).wait_recv()


def finish_kernel(costs_ref, gradient_ref, out_hbm, out_v, sem):
    copies = []
    for q in range(FBD // 8):
        for j in range(TILE):
            rows = pl.ds(q * 8 * TILE + j, 8, stride=TILE)
            value = gradient_ref[(j % 2) * PAIRS + j // 2, q * 8 : (q + 1) * 8]
            out_v[rows, :] = costs_ref[rows, :] - value
        rows = pl.ds(q * 8 * TILE, 8 * TILE)
        copies.append(pltpu.make_async_copy(out_v.at[rows], out_hbm.at[rows], sem.at[q]))
        copies[-1].start()
    for one in copies:
        one.wait()


def local(ny, nx, nz, duals, tiles, tile_rows, tile_cols, block_counts, probabilities, customer_map, costs):
    scen = duals.shape[0]
    bf16, f32 = jnp.bfloat16, jnp.float32
    part = PAIRS // 2
    vmem = pl.BlockSpec(memory_space=pltpu.VMEM)
    far = pl.BlockSpec(memory_space=pl.ANY)
    hbm = pl.BlockSpec(memory_space=pltpu.HBM)
    dma = pltpu.SemaphoreType.DMA
    sems = dma((2, len(CHUNKS), max(nx, ny)))
    deep = min(DEEP, scen)
    gradient = pl.pallas_call(
        functools.partial(exchange_kernel, ny, nx, nz, scen),
        out_shape=jax.ShapeDtypeStruct((TILE, FBD, LANES), f32),
        in_specs=[hbm] * 7,
        out_specs=far,
        scratch_shapes=[
            pltpu.VMEM(tile_rows.shape, jnp.int32),
            pltpu.VMEM(tile_cols.shape, jnp.int32),
            pltpu.SMEM((scen,), jnp.int32),
            pltpu.SMEM((scen,), f32),
            pltpu.SMEM(customer_map.shape, jnp.int32),
            pltpu.VMEM(duals.shape, bf16),
            pltpu.VMEM(tiles.shape, bf16),
            pltpu.VMEM((scen, nz, TILE, LANES), bf16),
            pltpu.VMEM((scen, nz, TILE, LANES), bf16),
            pltpu.VMEM((nz * FBD, SLOTS), bf16),
            pltpu.VMEM((deep, PAIRS * FBD, nz * LANES), bf16),
            pltpu.VMEM((deep, PAIRS * FBD, nz * LANES), bf16),
            pltpu.VMEM((nz * LANES, 2 * LANES), bf16),
            pltpu.VMEM((TILE, FBD, LANES), f32),
            pltpu.VMEM((PAIRS, FBD, LANES), f32),
            pltpu.VMEM((nx - 1, part // nx, FBD, LANES), f32),
            pltpu.VMEM((ny - 1, part // ny, FBD, LANES), f32),
            pltpu.VMEM((part // nx, FBD, LANES), f32),
            pltpu.VMEM((part // ny, FBD, LANES), f32),
            pltpu.VMEM((ny - 1, part // nx // ny, FBD, LANES), f32),
            pltpu.VMEM((nx - 1, part // nx // ny, FBD, LANES), f32),
            pltpu.VMEM((part // nx // ny, FBD, LANES), f32),
            pltpu.VMEM((part // nx // ny, FBD, LANES), f32),
            dma((5,)),
            dma,
            dma((scen,)),
            dma((scen, nz)),
            dma((scen, nz)),
            dma((2, len(CHUNKS))),
            dma((2, len(CHUNKS))),
        ]
        + [sems] * 10
        + [dma((2, len(CHUNKS)))],
        compiler_params=pltpu.CompilerParams(
            collective_id=0, has_side_effects=True, vmem_limit_bytes=62 * 2**20
        ),
        name="exchange",
    )(duals, tiles, tile_rows, tile_cols, block_counts.reshape(scen), probabilities, customer_map)
    return pl.pallas_call(
        finish_kernel,
        out_shape=jax.ShapeDtypeStruct(costs.shape, f32),
        in_specs=[vmem, vmem],
        out_specs=hbm,
        scratch_shapes=[pltpu.VMEM(costs.shape, f32), dma((FBD // 8,))],
        compiler_params=pltpu.CompilerParams(vmem_limit_bytes=32 * 2**20),
        name="finish",
    )(costs, gradient)


def solution(mesh):
    nz = mesh.shape["fac"]
    chips = mesh.shape["scen"] // 2
    side = 1
    while side * side < chips:
        side += 1
    in_specs = (
        P("scen", "fac", None),
        P("scen", "fac", None),
        P("scen", "fac"),
        P("scen", "fac"),
        P("scen", "fac"),
        P("scen"),
        P(),
        P("fac", None),
    )
    out_specs = P("fac", None)
    return jax.shard_map(
        functools.partial(local, side, side, nz),
        mesh=mesh,
        in_specs=in_specs,
        out_specs=out_specs,
        check_vma=False,
    )
```

```python
import functools

import jax
import jax.numpy as jnp
from jax import lax
from jax.experimental import pallas as pl
from jax.experimental.pallas import tpu as pltpu
from jax.sharding import PartitionSpec as P

TILE = 64
FBD = 40
SLOTS = 128
LANES = 128
PAIRS = TILE // 2
WIDE = 16
DEEP = 5
TOP = 32767.0
MESH = pl.DeviceIdType.MESH


def coded(value):
    most = jnp.max(jnp.abs(value), axis=0, keepdims=True)
    steps = value * (TOP / jnp.maximum(most, 1e-30))
    return jnp.floor(steps + 0.5).astype(jnp.int32).astype(jnp.int16), most * (1.0 / TOP)


def decoded(steps, scale):
    return steps.astype(jnp.int32).astype(jnp.float32) * scale


def exchange_kernel(
    ny,
    nx,
    nz,
    scen,
    duals_hbm,
    tiles_hbm,
    rows_hbm,
    cols_hbm,
    counts_hbm,
    prob_hbm,
    map_hbm,
    costs_hbm,
    out,
    out_scale,
    rows_ref,
    cols_ref,
    counts_ref,
    prob_ref,
    map_ref,
    duals_v,
    tiles_v,
    stage,
    land,
    selector,
    high,
    low,
    weights,
    acc,
    core_in,
    own_costs,
    r_out,
    r_out_scale,
    r_in,
    r_in_scale,
    last,
    last_scale,
    small_sem,
    duals_sem,
    tiles_sem,
    z_send,
    z_recv,
    c_send,
    c_recv,
    r_send,
    r_recv,
    rs_send,
    rs_recv,
    g_send,
    g_recv,
    gs_send,
    gs_recv,
    f_send,
    f_recv,
    fs_send,
    fs_recv,
    own_sem,
):
    sc = lax.axis_index("scen")
    me = lax.axis_index("fac")
    core = lax.rem(sc, 2)
    xx = lax.rem(lax.div(sc, 2), nx)
    yy = lax.div(sc, 2 * nx)
    chips = ny * nx
    chip = lax.div(sc, 2)

    def at(y, x, c):
        return (lax.rem(y, ny) * nx + lax.rem(x, nx)) * 2 + c

    sibling = (at(yy, xx, 1 - core), me)

    barrier = pltpu.get_barrier_semaphore()
    peers = [(sc, lax.rem(me + d, nz)) for d in range(1, nz)]
    peers += [(at(yy + e // nx, xx + e % nx, core), me) for e in range(1, chips)]
    peers.append(sibling)
    for one in peers:
        pl.semaphore_signal(barrier, inc=1, device_id=one, device_id_type=MESH)

    duals_copy = pltpu.make_async_copy(duals_hbm, duals_v, duals_sem)
    pairs = ((map_hbm, map_ref), (rows_hbm, rows_ref), (cols_hbm, cols_ref), (counts_hbm, counts_ref), (prob_hbm, prob_ref))
    smalls = [pltpu.make_async_copy(src, dst, small_sem.at[n]) for n, (src, dst) in enumerate(pairs)]
    smalls[0].start()
    duals_copy.start()
    for one in smalls[1:]:
        one.start()

    per = PAIRS // chips

    def costs_copy(n):
        j = 2 * (chip * per + n) + core
        return pltpu.make_async_copy(costs_hbm.at[:, j], own_costs.at[n], own_sem.at[2 + n])

    for n in range(per):
        costs_copy(n).start()

    def tiles_copy(s):
        return pltpu.make_async_copy(tiles_hbm.at[s], tiles_v.at[s], tiles_sem.at[s])

    @pl.loop(0, scen)
    def _(s):
        tiles_copy(s).start()

    weights[...] = jnp.zeros_like(weights)
    acc[...] = jnp.zeros_like(acc)
    for one in smalls:
        one.wait()

    owners = [map_ref[me * nz + k] for k in range(nz)]
    keep = [[jnp.where(owner == o, 1.0, 0.0) for owner in owners] for o in range(nz)]
    duals_copy.wait()

    @pl.loop(0, scen)
    def _(s):
        blocks = [duals_v[s, k * TILE : (k + 1) * TILE, :].astype(jnp.float32) for k in range(nz)]
        for o in range(nz):
            block = blocks[0] * keep[o][0]
            for k in range(1, nz):
                block = block + blocks[k] * keep[o][k]
            stage[s, o] = block.astype(jnp.bfloat16)

    def densify(s):
        slot = lax.rem(s, DEEP)
        position = lax.broadcasted_iota(jnp.int32, (1, SLOTS), 1)
        cells = rows_ref[pl.ds(s, 1), :] * FBD + cols_ref[pl.ds(s, 1), :]
        cells = jnp.where(position < counts_ref[s], cells, -1)
        cell_ids = lax.broadcasted_iota(jnp.int32, (nz * FBD, SLOTS), 0)
        selector[...] = jnp.where(cell_ids == cells, 1.0, 0.0).astype(jnp.bfloat16)
        tiles_copy(s).wait()
        for n in range(WIDE):
            block = tiles_v[s, :, n * 256 : (n + 1) * 256]
            dense = jnp.dot(selector[...], block, preferred_element_type=jnp.float32)
            for r in range(nz):
                part = dense[r * FBD : (r + 1) * FBD]
                both = jnp.concatenate([part[:, :LANES], part[:, LANES:]], axis=0)
                upper = both.astype(jnp.bfloat16)
                lower = (both - upper.astype(jnp.float32)).astype(jnp.bfloat16)
                high[slot, n * 80 : (n + 1) * 80, r * LANES : (r + 1) * LANES] = upper
                low[slot, n * 80 : (n + 1) * 80, r * LANES : (r + 1) * LANES] = lower

    densify(0)
    pl.semaphore_wait(barrier, len(peers))

    def z_copy(s, d):
        to = lax.rem(me + d, nz)
        return pltpu.make_async_remote_copy(
            src_ref=stage.at[s, to],
            dst_ref=land.at[s, me],
            send_sem=z_send.at[s, d],
            recv_sem=z_recv.at[s, d],
            device_id=(sc, to),
            device_id_type=MESH,
        )

    def z_arrival(s, d):
        source = lax.rem(me + nz - d, nz)
        return pltpu.make_async_remote_copy(
            src_ref=stage.at[s, source],
            dst_ref=land.at[s, source],
            send_sem=z_send.at[s, d],
            recv_sem=z_recv.at[s, d],
            device_id=(sc, source),
            device_id_type=MESH,
        )

    order = sorted(range(1, nz), key=lambda d: -min(d, nz - d))

    @pl.loop(0, scen)
    def _(s):
        for d in order:
            z_copy(s, d).start()
        land[s, me] = stage[s, me]

    @pl.loop(1, min(DEEP, scen))
    def _(s):
        densify(s)

    part = PAIRS // 2
    mine = core * PAIRS
    other = (1 - core) * PAIRS

    def core_copy(k):
        return pltpu.make_async_remote_copy(
            src_ref=acc.at[pl.ds(other + k * part, part)],
            dst_ref=core_in.at[pl.ds(k * part, part)],
            send_sem=c_send.at[k],
            recv_sem=c_recv.at[k],
            device_id=sibling,
            device_id_type=MESH,
        )

    @pl.loop(0, scen)
    def _(s):
        slot = lax.rem(s, DEEP)
        for d in range(1, nz):
            z_arrival(s, d).wait_recv()
        for r in range(nz):
            block = land[s, r]
            weights[r * LANES : r * LANES + TILE, :LANES] = block
            weights[r * LANES + TILE : (r + 1) * LANES, LANES:] = block

        scale = prob_ref[s]
        for n in range(4):
            rows = slice(n * 320, (n + 1) * 320)
            value = jnp.dot(high[slot, rows], weights[...], preferred_element_type=jnp.float32)
            value = value + jnp.dot(low[slot, rows], weights[...], preferred_element_type=jnp.float32)
            value = value * scale
            acc[n * 8 : (n + 1) * 8] += value[:, :LANES].reshape(8, FBD, LANES)
            acc[PAIRS + n * 8 : PAIRS + (n + 1) * 8] += value[:, LANES:].reshape(8, FBD, LANES)
            if n % 2:

                @pl.when(s == scen - 1)
                def _():
                    core_copy(n // 2).start()

        @pl.when(s < scen - DEEP)
        def _():
            densify(s + DEEP)

    def remote(src, dst, send, recv, to):
        return pltpu.make_async_remote_copy(
            src_ref=src, dst_ref=dst, send_sem=send, recv_sem=recv, device_id=to, device_id_type=MESH
        )

    def there(e):
        return lax.rem(yy + e // nx, ny) * nx + lax.rem(xx + e % nx, nx)

    def whence(e):
        return lax.rem(yy + ny - e // nx, ny) * nx + lax.rem(xx + nx - e % nx, nx)

    def r_copies(e):
        to = there(e)
        device = (to * 2 + core, me)
        return (
            remote(r_out.at[to], r_in.at[e], r_send.at[e], r_recv.at[e], device),
            remote(r_out_scale.at[to], r_in_scale.at[e], rs_send.at[e], rs_recv.at[e], device),
        )

    def g_copies(e, shard):
        device = (there(e) * 2 + core, me)
        return (
            remote(last, out.at[shard], g_send.at[e], g_recv.at[e], device),
            remote(last_scale, out_scale.at[shard], gs_send.at[e], gs_recv.at[e], device),
        )

    def f_copies(e, shard):
        return (
            remote(out.at[shard], out.at[shard], f_send.at[e], f_recv.at[e], sibling),
            remote(out_scale.at[shard], out_scale.at[shard], fs_send.at[e], fs_recv.at[e], sibling),
        )

    hops = sorted(range(1, chips), key=lambda e: -min(e // nx, ny - e // nx) - min(e % nx, nx - e % nx))
    own = (
        pltpu.make_async_copy(last, out.at[core * chips + chip], own_sem.at[0]),
        pltpu.make_async_copy(last_scale, out_scale.at[core * chips + chip], own_sem.at[1]),
    )
    rows = per * FBD

    def wide(scale):
        return jnp.broadcast_to(scale, (8, LANES))

    for k in range(2):
        core_copy(k).wait_recv()
    for e in hops:
        to = there(e)
        value = acc[pl.ds(mine + to * per, per)] + core_in[pl.ds(to * per, per)]
        steps, scale = coded(value.reshape(rows, LANES))
        r_out[to] = steps
        r_out_scale[to] = wide(scale)
        for one in r_copies(e):
            one.start()
    total = acc[pl.ds(mine + chip * per, per)] + core_in[pl.ds(chip * per, per)]
    total = total.reshape(rows, LANES)
    for n in range(per):
        costs_copy(n).wait()
    for e in hops:
        for one in r_copies(e):
            one.wait_recv()
        total = total + decoded(r_in[e], r_in_scale[e, :1])
    steps, scale = coded(own_costs[...].reshape(rows, LANES) - total)
    last[...] = steps
    last_scale[...] = wide(scale)
    for e in hops:
        for one in g_copies(e, core * chips + chip):
            one.start()
    for one in own:
        one.start()
    for one in own:
        one.wait()
    for one in f_copies(0, core * chips + chip):
        one.start()
    for e in reversed(hops):
        shard = core * chips + whence(e)
        for one in g_copies(e, shard):
            one.wait_recv()
        for one in f_copies(e, shard):
            one.start()

    @pl.loop(0, scen)
    def _(s):
        for d in range(1, nz):
            z_copy(s, d).wait_send()

    for k in range(2):
        core_copy(k).wait_send()
    for e in hops:
        for one in r_copies(e) + g_copies(e, core * chips + chip):
            one.wait_send()
    for e in range(chips):
        shard = whence(e)
        for one in f_copies(e, core * chips + shard):
            one.wait_send()
        for one in f_copies(e, (1 - core) * chips + shard):
            one.wait_recv()


def finish_kernel(steps_ref, scale_ref, out_ref):
    shards = steps_ref.shape[0] // 2
    per = PAIRS // shards
    for q in range(2 * shards):
        value = decoded(steps_ref[q], scale_ref[q, :1])
        for n in range(per):
            j = 2 * ((q % shards) * per + n) + q // shards
            out_ref[pl.ds(j, FBD, stride=TILE), :] = value[n * FBD : (n + 1) * FBD]


def local(ny, nx, nz, duals, tiles, tile_rows, tile_cols, block_counts, probabilities, customer_map, costs):
    scen = duals.shape[0]
    bf16, f32 = jnp.bfloat16, jnp.float32
    chips = ny * nx
    rows = PAIRS // chips * FBD
    i16 = jnp.int16
    vmem = pl.BlockSpec(memory_space=pltpu.VMEM)
    far = pl.BlockSpec(memory_space=pl.ANY)
    hbm = pl.BlockSpec(memory_space=pltpu.HBM)
    dma = pltpu.SemaphoreType.DMA
    sems = dma((chips,))
    deep = min(DEEP, scen)
    steps, scale = pl.pallas_call(
        functools.partial(exchange_kernel, ny, nx, nz, scen),
        out_shape=(
            jax.ShapeDtypeStruct((2 * chips, rows, LANES), i16),
            jax.ShapeDtypeStruct((2 * chips, 8, LANES), f32),
        ),
        in_specs=[hbm] * 8,
        out_specs=(far, far),
        scratch_shapes=[
            pltpu.VMEM(tile_rows.shape, jnp.int32),
            pltpu.VMEM(tile_cols.shape, jnp.int32),
            pltpu.SMEM((scen,), jnp.int32),
            pltpu.SMEM((scen,), f32),
            pltpu.SMEM(customer_map.shape, jnp.int32),
            pltpu.VMEM(duals.shape, bf16),
            pltpu.VMEM(tiles.shape, bf16),
            pltpu.VMEM((scen, nz, TILE, LANES), bf16),
            pltpu.VMEM((scen, nz, TILE, LANES), bf16),
            pltpu.VMEM((nz * FBD, SLOTS), bf16),
            pltpu.VMEM((deep, PAIRS * FBD, nz * LANES), bf16),
            pltpu.VMEM((deep, PAIRS * FBD, nz * LANES), bf16),
            pltpu.VMEM((nz * LANES, 2 * LANES), bf16),
            pltpu.VMEM((TILE, FBD, LANES), f32),
            pltpu.VMEM((PAIRS, FBD, LANES), f32),
            pltpu.VMEM((PAIRS // chips, FBD, LANES), f32),
            pltpu.VMEM((chips, rows, LANES), i16),
            pltpu.VMEM((chips, 8, LANES), f32),
            pltpu.VMEM((chips, rows, LANES), i16),
            pltpu.VMEM((chips, 8, LANES), f32),
            pltpu.VMEM((rows, LANES), i16),
            pltpu.VMEM((8, LANES), f32),
            dma((5,)),
            dma,
            dma((scen,)),
            dma((scen, nz)),
            dma((scen, nz)),
            dma((2,)),
            dma((2,)),
        ]
        + [sems] * 12
        + [dma((2 + PAIRS // chips,))],
        compiler_params=pltpu.CompilerParams(
            collective_id=0, has_side_effects=True, vmem_limit_bytes=62 * 2**20
        ),
        name="exchange",
    )(duals, tiles, tile_rows, tile_cols, block_counts.reshape(scen), probabilities, customer_map, costs.reshape(FBD, TILE, LANES))
    return pl.pallas_call(
        finish_kernel,
        out_shape=jax.ShapeDtypeStruct(costs.shape, f32),
        in_specs=[vmem, vmem],
        out_specs=vmem,
        compiler_params=pltpu.CompilerParams(vmem_limit_bytes=32 * 2**20),
        name="finish",
    )(steps, scale)


def solution(mesh):
    nz = mesh.shape["fac"]
    chips = mesh.shape["scen"] // 2
    side = 1
    while side * side < chips:
        side += 1
    in_specs = (
        P("scen", "fac", None),
        P("scen", "fac", None),
        P("scen", "fac"),
        P("scen", "fac"),
        P("scen", "fac"),
        P("scen"),
        P(),
        P("fac", None),
    )
    out_specs = P("fac", None)
    return jax.shard_map(
        functools.partial(local, side, side, nz),
        mesh=mesh,
        in_specs=in_specs,
        out_specs=out_specs,
        check_vma=False,
    )
```

```python
import functools

import jax
import jax.numpy as jnp
from jax import lax
from jax.experimental import pallas as pl
from jax.experimental.pallas import tpu as pltpu
from jax.sharding import PartitionSpec as P

TILE = 64
FBD = 40
SLOTS = 128
LANES = 128
PAIRS = TILE // 2
WIDE = 16
DEEP = 5
TOP = 32000.0
MARK = 16
GROUP = 5
MESH = pl.DeviceIdType.MESH


def coded(value):
    most = jnp.max(jnp.abs(value), axis=0, keepdims=True)
    power = jnp.ceil(jnp.log2(jnp.maximum(most, 1e-30)))
    steps = jnp.floor(value * (jnp.exp2(-power) * TOP) + 0.5)
    mark = jnp.broadcast_to(power, (MARK, LANES))
    return jnp.concatenate([steps, mark], axis=0).astype(jnp.int32).astype(jnp.int16)


def decoded(message):
    wide = message.astype(jnp.int32).astype(jnp.float32)
    return wide[:-MARK] * (jnp.exp2(wide[-MARK : 1 - MARK]) * (1.0 / TOP))


def exchange_kernel(
    ny,
    nx,
    nz,
    scen,
    duals_hbm,
    tiles_hbm,
    rows_hbm,
    cols_hbm,
    counts_hbm,
    prob_hbm,
    map_hbm,
    costs_hbm,
    out_hbm,
    rows_ref,
    cols_ref,
    counts_ref,
    prob_ref,
    map_ref,
    duals_v,
    tiles_v,
    stage,
    land,
    selector,
    high,
    low,
    weights,
    acc,
    core_in,
    own_costs,
    r_out,
    r_in,
    last,
    gathered,
    out_v,
    small_sem,
    duals_sem,
    tiles_sem,
    z_send,
    z_recv,
    c_send,
    c_recv,
    r_send,
    r_recv,
    g_send,
    g_recv,
    f_send,
    f_recv,
    own_sem,
    out_sem,
):
    sc = lax.axis_index("scen")
    me = lax.axis_index("fac")
    core = lax.rem(sc, 2)
    xx = lax.rem(lax.div(sc, 2), nx)
    yy = lax.div(sc, 2 * nx)
    chips = ny * nx
    chip = lax.div(sc, 2)

    def at(y, x, c):
        return (lax.rem(y, ny) * nx + lax.rem(x, nx)) * 2 + c

    sibling = (at(yy, xx, 1 - core), me)

    barrier = pltpu.get_barrier_semaphore()
    peers = [(sc, lax.rem(me + d, nz)) for d in range(1, nz)]
    peers += [(at(yy + e // nx, xx + e % nx, core), me) for e in range(1, chips)]
    peers.append(sibling)
    for one in peers:
        pl.semaphore_signal(barrier, inc=1, device_id=one, device_id_type=MESH)

    duals_copy = pltpu.make_async_copy(duals_hbm, duals_v, duals_sem)
    pairs = ((map_hbm, map_ref), (rows_hbm, rows_ref), (cols_hbm, cols_ref), (counts_hbm, counts_ref), (prob_hbm, prob_ref))
    smalls = [pltpu.make_async_copy(src, dst, small_sem.at[n]) for n, (src, dst) in enumerate(pairs)]
    smalls[0].start()
    duals_copy.start()
    for one in smalls[1:]:
        one.start()

    per = PAIRS // chips

    def costs_copy(n):
        j = 2 * (chip * per + n) + core
        return pltpu.make_async_copy(costs_hbm.at[:, j], own_costs.at[n], own_sem.at[n])

    for n in range(per):
        costs_copy(n).start()

    def tiles_copy(s):
        return pltpu.make_async_copy(tiles_hbm.at[s], tiles_v.at[s], tiles_sem.at[s])

    @pl.loop(0, scen)
    def _(s):
        tiles_copy(s).start()

    weights[...] = jnp.zeros_like(weights)
    acc[...] = jnp.zeros_like(acc)
    for one in smalls:
        one.wait()

    owners = [map_ref[me * nz + k] for k in range(nz)]
    keep = [[jnp.where(owner == o, 1.0, 0.0) for owner in owners] for o in range(nz)]
    duals_copy.wait()

    @pl.loop(0, scen)
    def _(s):
        blocks = [duals_v[s, k * TILE : (k + 1) * TILE, :].astype(jnp.float32) for k in range(nz)]
        for o in range(nz):
            block = blocks[0] * keep[o][0]
            for k in range(1, nz):
                block = block + blocks[k] * keep[o][k]
            stage[s, o] = block.astype(jnp.bfloat16)

    def densify(s):
        slot = lax.rem(s, DEEP)
        position = lax.broadcasted_iota(jnp.int32, (1, SLOTS), 1)
        cells = rows_ref[pl.ds(s, 1), :] * FBD + cols_ref[pl.ds(s, 1), :]
        cells = jnp.where(position < counts_ref[s], cells, -1)
        cell_ids = lax.broadcasted_iota(jnp.int32, (nz * FBD, SLOTS), 0)
        selector[...] = jnp.where(cell_ids == cells, 1.0, 0.0).astype(jnp.bfloat16)
        tiles_copy(s).wait()
        for n in range(WIDE):
            block = tiles_v[s, :, n * 256 : (n + 1) * 256]
            dense = jnp.dot(selector[...], block, preferred_element_type=jnp.float32)
            for r in range(nz):
                part = dense[r * FBD : (r + 1) * FBD]
                both = jnp.concatenate([part[:, :LANES], part[:, LANES:]], axis=0)
                upper = both.astype(jnp.bfloat16)
                lower = (both - upper.astype(jnp.float32)).astype(jnp.bfloat16)
                high[slot, n * 80 : (n + 1) * 80, r * LANES : (r + 1) * LANES] = upper
                low[slot, n * 80 : (n + 1) * 80, r * LANES : (r + 1) * LANES] = lower

    densify(0)
    pl.semaphore_wait(barrier, len(peers))

    def z_copy(s, d):
        to = lax.rem(me + d, nz)
        return pltpu.make_async_remote_copy(
            src_ref=stage.at[s, to],
            dst_ref=land.at[s, me],
            send_sem=z_send.at[s, d],
            recv_sem=z_recv.at[s, d],
            device_id=(sc, to),
            device_id_type=MESH,
        )

    def z_arrival(s, d):
        source = lax.rem(me + nz - d, nz)
        return pltpu.make_async_remote_copy(
            src_ref=stage.at[s, source],
            dst_ref=land.at[s, source],
            send_sem=z_send.at[s, d],
            recv_sem=z_recv.at[s, d],
            device_id=(sc, source),
            device_id_type=MESH,
        )

    order = sorted(range(1, nz), key=lambda d: -min(d, nz - d))

    @pl.loop(0, scen)
    def _(s):
        for d in order:
            z_copy(s, d).start()
        land[s, me] = stage[s, me]

    @pl.loop(1, min(DEEP, scen))
    def _(s):
        densify(s)

    part = PAIRS // 4
    mine = core * PAIRS
    other = (1 - core) * PAIRS

    def core_copy(k):
        return pltpu.make_async_remote_copy(
            src_ref=acc.at[pl.ds(other + k * part, part)],
            dst_ref=core_in.at[pl.ds(k * part, part)],
            send_sem=c_send.at[k],
            recv_sem=c_recv.at[k],
            device_id=sibling,
            device_id_type=MESH,
        )

    @pl.loop(0, scen)
    def _(s):
        slot = lax.rem(s, DEEP)
        for d in range(1, nz):
            z_arrival(s, d).wait_recv()
        for r in range(nz):
            block = land[s, r]
            weights[r * LANES : r * LANES + TILE, :LANES] = block
            weights[r * LANES + TILE : (r + 1) * LANES, LANES:] = block

        scale = prob_ref[s]
        for n in range(4):
            rows = slice(n * 320, (n + 1) * 320)
            value = jnp.dot(high[slot, rows], weights[...], preferred_element_type=jnp.float32)
            value = value + jnp.dot(low[slot, rows], weights[...], preferred_element_type=jnp.float32)
            value = value * scale
            acc[n * 8 : (n + 1) * 8] += value[:, :LANES].reshape(8, FBD, LANES)
            acc[PAIRS + n * 8 : PAIRS + (n + 1) * 8] += value[:, LANES:].reshape(8, FBD, LANES)

            @pl.when(s == scen - 1)
            def _():
                core_copy(n).start()

        @pl.when(s < scen - DEEP)
        def _():
            densify(s + DEEP)

    def remote(src, dst, send, recv, to):
        return pltpu.make_async_remote_copy(
            src_ref=src, dst_ref=dst, send_sem=send, recv_sem=recv, device_id=to, device_id_type=MESH
        )

    def there(e):
        return lax.rem(yy + e // nx, ny) * nx + lax.rem(xx + e % nx, nx)

    def whence(e):
        return lax.rem(yy + ny - e // nx, ny) * nx + lax.rem(xx + nx - e % nx, nx)

    def r_copy(e):
        to = there(e)
        return remote(r_out.at[to], r_in.at[e], r_send.at[e], r_recv.at[e], (to * 2 + core, me))

    def g_copy(e, shard):
        return remote(last, gathered.at[shard], g_send.at[e], g_recv.at[e], (there(e) * 2 + core, me))

    def f_copy(e, src, shard):
        return remote(src, gathered.at[shard], f_send.at[e], f_recv.at[e], sibling)

    hops = sorted(range(1, chips), key=lambda e: -min(e // nx, ny - e // nx) - min(e % nx, nx - e % nx))
    rows = per * FBD

    def place(message, half, where):
        value = decoded(message)
        for n in range(per):
            j = 2 * (where * per + n) + half
            out_v[pl.ds(j, FBD, stride=TILE), :] = value[n * FBD : (n + 1) * FBD]

    for k in range(4):
        core_copy(k).wait_recv()
    for first in range(0, chips - 1, GROUP):
        group = hops[first : first + GROUP]
        values = [acc[pl.ds(mine + there(e) * per, per)] + core_in[pl.ds(there(e) * per, per)] for e in group]
        messages = [coded(value.reshape(rows, LANES)) for value in values]
        for e, message in zip(group, messages):
            r_out[there(e)] = message
        for e in group:
            r_copy(e).start()
    total = acc[pl.ds(mine + chip * per, per)] + core_in[pl.ds(chip * per, per)]
    for n in range(per):
        costs_copy(n).wait()
    total = (own_costs[...] - total).reshape(rows, LANES)
    for e in hops:
        r_copy(e).wait_recv()
        total = total - decoded(r_in[e])
    shard = core * chips + chip
    last[...] = coded(total)
    for e in hops:
        g_copy(e, shard).start()
    f_copy(0, last, shard).start()
    place(last[...], core, chip)
    for e in reversed(hops):
        shard = core * chips + whence(e)
        g_copy(e, shard).wait_recv()
        f_copy(e, gathered.at[shard], shard).start()
        place(gathered[shard], core, whence(e))
    for e in [0] + hops[::-1]:
        shard = (1 - core) * chips + whence(e)
        f_copy(e, last, shard).wait_recv()
        place(gathered[shard], 1 - core, whence(e))
    out_copy = pltpu.make_async_copy(out_v, out_hbm, out_sem)
    out_copy.start()

    @pl.loop(0, scen)
    def _(s):
        for d in range(1, nz):
            z_copy(s, d).wait_send()

    for k in range(4):
        core_copy(k).wait_send()
    for e in hops:
        r_copy(e).wait_send()
        g_copy(e, core * chips + chip).wait_send()
    for e in range(chips):
        f_copy(e, last, core * chips + chip).wait_send()
    out_copy.wait()


def local(ny, nx, nz, duals, tiles, tile_rows, tile_cols, block_counts, probabilities, customer_map, costs):
    scen = duals.shape[0]
    bf16, f32 = jnp.bfloat16, jnp.float32
    chips = ny * nx
    rows = PAIRS // chips * FBD
    i16 = jnp.int16
    hbm = pl.BlockSpec(memory_space=pltpu.HBM)
    dma = pltpu.SemaphoreType.DMA
    sems = dma((chips,))
    deep = min(DEEP, scen)
    return pl.pallas_call(
        functools.partial(exchange_kernel, ny, nx, nz, scen),
        out_shape=jax.ShapeDtypeStruct(costs.shape, f32),
        in_specs=[hbm] * 8,
        out_specs=hbm,
        scratch_shapes=[
            pltpu.VMEM(tile_rows.shape, jnp.int32),
            pltpu.VMEM(tile_cols.shape, jnp.int32),
            pltpu.SMEM((scen,), jnp.int32),
            pltpu.SMEM((scen,), f32),
            pltpu.SMEM(customer_map.shape, jnp.int32),
            pltpu.VMEM(duals.shape, bf16),
            pltpu.VMEM(tiles.shape, bf16),
            pltpu.VMEM((scen, nz, TILE, LANES), bf16),
            pltpu.VMEM((scen, nz, TILE, LANES), bf16),
            pltpu.VMEM((nz * FBD, SLOTS), bf16),
            pltpu.VMEM((deep, PAIRS * FBD, nz * LANES), bf16),
            pltpu.VMEM((deep, PAIRS * FBD, nz * LANES), bf16),
            pltpu.VMEM((nz * LANES, 2 * LANES), bf16),
            pltpu.VMEM((TILE, FBD, LANES), f32),
            pltpu.VMEM((PAIRS, FBD, LANES), f32),
            pltpu.VMEM((PAIRS // chips, FBD, LANES), f32),
            pltpu.VMEM((chips, rows + MARK, LANES), i16),
            pltpu.VMEM((chips, rows + MARK, LANES), i16),
            pltpu.VMEM((rows + MARK, LANES), i16),
            pltpu.VMEM((2 * chips, rows + MARK, LANES), i16),
            pltpu.VMEM(costs.shape, f32),
            dma((5,)),
            dma,
            dma((scen,)),
            dma((scen, nz)),
            dma((scen, nz)),
            dma((4,)),
            dma((4,)),
        ]
        + [sems] * 6
        + [dma((PAIRS // chips,)), dma],
        compiler_params=pltpu.CompilerParams(
            collective_id=0, has_side_effects=True, vmem_limit_bytes=62 * 2**20
        ),
        name="exchange",
    )(duals, tiles, tile_rows, tile_cols, block_counts.reshape(scen), probabilities, customer_map, costs.reshape(FBD, TILE, LANES))


def solution(mesh):
    nz = mesh.shape["fac"]
    chips = mesh.shape["scen"] // 2
    side = 1
    while side * side < chips:
        side += 1
    in_specs = (
        P("scen", "fac", None),
        P("scen", "fac", None),
        P("scen", "fac"),
        P("scen", "fac"),
        P("scen", "fac"),
        P("scen"),
        P(),
        P("fac", None),
    )
    out_specs = P("fac", None)
    return jax.shard_map(
        functools.partial(local, side, side, nz),
        mesh=mesh,
        in_specs=in_specs,
        out_specs=out_specs,
        check_vma=False,
    )
```

```python
import functools

import jax
import jax.numpy as jnp
from jax import lax
from jax.experimental import pallas as pl
from jax.experimental.pallas import tpu as pltpu
from jax.sharding import PartitionSpec as P

TILE = 64
FBD = 40
SLOTS = 128
LANES = 128
PAIRS = TILE // 2
WIDE = 16
DEEP = 5
TOP = 32000.0
MARK = 16
GROUP = 5
MESH = pl.DeviceIdType.MESH


def coded(value):
    most = jnp.max(jnp.abs(value), axis=0, keepdims=True)
    power = jnp.ceil(jnp.log2(jnp.maximum(most, 1e-30)))
    steps = jnp.floor(value * (jnp.exp2(-power) * TOP) + 0.5)
    mark = jnp.broadcast_to(power, (MARK, LANES))
    return jnp.concatenate([steps, mark], axis=0).astype(jnp.int32).astype(jnp.int16)


def decoded(message):
    wide = message.astype(jnp.int32).astype(jnp.float32)
    return wide[:-MARK] * (jnp.exp2(wide[-MARK : 1 - MARK]) * (1.0 / TOP))


def by_eight(value):
    count = value.shape[0]
    return jnp.concatenate([value[m, c : c + 8] for c in range(0, FBD, 8) for m in range(count)], axis=0)


def exchange_kernel(
    ny,
    nx,
    nz,
    scen,
    duals_hbm,
    tiles_hbm,
    rows_hbm,
    cols_hbm,
    counts_hbm,
    prob_hbm,
    map_hbm,
    costs_hbm,
    out,
    rows_ref,
    cols_ref,
    counts_ref,
    prob_ref,
    map_ref,
    duals_v,
    tiles_v,
    stage,
    land,
    selector,
    high,
    low,
    weights,
    acc,
    core_in,
    own_costs,
    r_out,
    r_in,
    last,
    gathered,
    small_sem,
    duals_sem,
    tiles_sem,
    z_send,
    z_recv,
    c_send,
    c_recv,
    r_send,
    r_recv,
    g_send,
    g_recv,
    f_send,
    f_recv,
    own_sem,
    out_sem,
):
    sc = lax.axis_index("scen")
    me = lax.axis_index("fac")
    core = lax.rem(sc, 2)
    xx = lax.rem(lax.div(sc, 2), nx)
    yy = lax.div(sc, 2 * nx)
    chips = ny * nx
    chip = lax.div(sc, 2)

    def at(y, x, c):
        return (lax.rem(y, ny) * nx + lax.rem(x, nx)) * 2 + c

    sibling = (at(yy, xx, 1 - core), me)

    barrier = pltpu.get_barrier_semaphore()
    peers = [(sc, lax.rem(me + d, nz)) for d in range(1, nz)]
    peers += [(at(yy + e // nx, xx + e % nx, core), me) for e in range(1, chips)]
    peers.append(sibling)
    for one in peers:
        pl.semaphore_signal(barrier, inc=1, device_id=one, device_id_type=MESH)

    duals_copy = pltpu.make_async_copy(duals_hbm, duals_v, duals_sem)
    pairs = ((map_hbm, map_ref), (rows_hbm, rows_ref), (cols_hbm, cols_ref), (counts_hbm, counts_ref), (prob_hbm, prob_ref))
    smalls = [pltpu.make_async_copy(src, dst, small_sem.at[n]) for n, (src, dst) in enumerate(pairs)]
    smalls[0].start()
    duals_copy.start()
    for one in smalls[1:]:
        one.start()

    per = PAIRS // chips

    def costs_copy(n):
        j = 2 * (chip * per + n) + core
        return pltpu.make_async_copy(costs_hbm.at[:, j], own_costs.at[n], own_sem.at[n])

    for n in range(per):
        costs_copy(n).start()

    def tiles_copy(s):
        return pltpu.make_async_copy(tiles_hbm.at[s], tiles_v.at[s], tiles_sem.at[s])

    @pl.loop(0, scen)
    def _(s):
        tiles_copy(s).start()

    weights[...] = jnp.zeros_like(weights)
    acc[...] = jnp.zeros_like(acc)
    for one in smalls:
        one.wait()

    owners = [map_ref[me * nz + k] for k in range(nz)]
    keep = [[jnp.where(owner == o, 1.0, 0.0) for owner in owners] for o in range(nz)]
    duals_copy.wait()

    @pl.loop(0, scen)
    def _(s):
        blocks = [duals_v[s, k * TILE : (k + 1) * TILE, :].astype(jnp.float32) for k in range(nz)]
        for o in range(nz):
            block = blocks[0] * keep[o][0]
            for k in range(1, nz):
                block = block + blocks[k] * keep[o][k]
            stage[s, o] = block.astype(jnp.bfloat16)

    def densify(s):
        slot = lax.rem(s, DEEP)
        position = lax.broadcasted_iota(jnp.int32, (1, SLOTS), 1)
        cells = rows_ref[pl.ds(s, 1), :] * FBD + cols_ref[pl.ds(s, 1), :]
        cells = jnp.where(position < counts_ref[s], cells, -1)
        cell_ids = lax.broadcasted_iota(jnp.int32, (nz * FBD, SLOTS), 0)
        selector[...] = jnp.where(cell_ids == cells, 1.0, 0.0).astype(jnp.bfloat16)
        tiles_copy(s).wait()
        for n in range(WIDE):
            block = tiles_v[s, :, n * 256 : (n + 1) * 256]
            dense = jnp.dot(selector[...], block, preferred_element_type=jnp.float32)
            for r in range(nz):
                part = dense[r * FBD : (r + 1) * FBD]
                both = jnp.concatenate([part[:, :LANES], part[:, LANES:]], axis=0)
                upper = both.astype(jnp.bfloat16)
                lower = (both - upper.astype(jnp.float32)).astype(jnp.bfloat16)
                high[slot, n * 80 : (n + 1) * 80, r * LANES : (r + 1) * LANES] = upper
                low[slot, n * 80 : (n + 1) * 80, r * LANES : (r + 1) * LANES] = lower

    densify(0)
    pl.semaphore_wait(barrier, len(peers))

    def z_copy(s, d):
        to = lax.rem(me + d, nz)
        return pltpu.make_async_remote_copy(
            src_ref=stage.at[s, to],
            dst_ref=land.at[s, me],
            send_sem=z_send.at[s, d],
            recv_sem=z_recv.at[s, d],
            device_id=(sc, to),
            device_id_type=MESH,
        )

    def z_arrival(s, d):
        source = lax.rem(me + nz - d, nz)
        return pltpu.make_async_remote_copy(
            src_ref=stage.at[s, source],
            dst_ref=land.at[s, source],
            send_sem=z_send.at[s, d],
            recv_sem=z_recv.at[s, d],
            device_id=(sc, source),
            device_id_type=MESH,
        )

    order = sorted(range(1, nz), key=lambda d: -min(d, nz - d))

    @pl.loop(0, scen)
    def _(s):
        for d in order:
            z_copy(s, d).start()
        land[s, me] = stage[s, me]

    @pl.loop(1, min(DEEP, scen))
    def _(s):
        densify(s)

    part = PAIRS // 2
    mine = core * PAIRS
    other = (1 - core) * PAIRS

    def core_copy(k):
        return pltpu.make_async_remote_copy(
            src_ref=acc.at[pl.ds(other + k * part, part)],
            dst_ref=core_in.at[pl.ds(k * part, part)],
            send_sem=c_send.at[k],
            recv_sem=c_recv.at[k],
            device_id=sibling,
            device_id_type=MESH,
        )

    @pl.loop(0, scen)
    def _(s):
        slot = lax.rem(s, DEEP)
        for d in range(1, nz):
            z_arrival(s, d).wait_recv()
        for r in range(nz):
            block = land[s, r]
            weights[r * LANES : r * LANES + TILE, :LANES] = block
            weights[r * LANES + TILE : (r + 1) * LANES, LANES:] = block

        scale = prob_ref[s]
        for n in range(4):
            rows = slice(n * 320, (n + 1) * 320)
            value = jnp.dot(high[slot, rows], weights[...], preferred_element_type=jnp.float32)
            value = value + jnp.dot(low[slot, rows], weights[...], preferred_element_type=jnp.float32)
            value = value * scale
            acc[n * 8 : (n + 1) * 8] += value[:, :LANES].reshape(8, FBD, LANES)
            acc[PAIRS + n * 8 : PAIRS + (n + 1) * 8] += value[:, LANES:].reshape(8, FBD, LANES)
            if n % 2:

                @pl.when(s == scen - 1)
                def _():
                    core_copy(n // 2).start()

        @pl.when(s < scen - DEEP)
        def _():
            densify(s + DEEP)

    def remote(src, dst, send, recv, to):
        return pltpu.make_async_remote_copy(
            src_ref=src, dst_ref=dst, send_sem=send, recv_sem=recv, device_id=to, device_id_type=MESH
        )

    def there(e):
        return lax.rem(yy + e // nx, ny) * nx + lax.rem(xx + e % nx, nx)

    def whence(e):
        return lax.rem(yy + ny - e // nx, ny) * nx + lax.rem(xx + nx - e % nx, nx)

    def r_copy(e):
        to = there(e)
        return remote(r_out.at[to], r_in.at[e], r_send.at[e], r_recv.at[e], (to * 2 + core, me))

    def g_copy(e, shard):
        return remote(last, gathered.at[shard], g_send.at[e], g_recv.at[e], (there(e) * 2 + core, me))

    def f_copy(e, src, shard):
        return remote(src, out.at[shard], f_send.at[e], f_recv.at[e], sibling)

    def out_copy(e, src, shard):
        return pltpu.make_async_copy(src, out.at[shard], out_sem.at[e])

    hops = sorted(range(1, chips), key=lambda e: -min(e // nx, ny - e // nx) - min(e % nx, nx - e % nx))
    for k in range(2):
        core_copy(k).wait_recv()
    for first in range(0, chips - 1, GROUP):
        group = hops[first : first + GROUP]
        values = [acc[pl.ds(mine + there(e) * per, per)] + core_in[pl.ds(there(e) * per, per)] for e in group]
        messages = [coded(by_eight(value)) for value in values]
        for e, message in zip(group, messages):
            r_out[there(e)] = message
        for e in group:
            r_copy(e).start()
    total = acc[pl.ds(mine + chip * per, per)] + core_in[pl.ds(chip * per, per)]
    for n in range(per):
        costs_copy(n).wait()
    total = by_eight(own_costs[...] - total)
    for e in hops:
        r_copy(e).wait_recv()
        total = total - decoded(r_in[e])
    shard = core * chips + chip
    last[...] = coded(total)
    for e in hops:
        g_copy(e, shard).start()
    f_copy(0, last, shard).start()
    out_copy(0, last, shard).start()
    for e in reversed(hops):
        shard = core * chips + whence(e)
        g_copy(e, shard).wait_recv()
        f_copy(e, gathered.at[shard], shard).start()
        out_copy(e, gathered.at[shard], shard).start()

    @pl.loop(0, scen)
    def _(s):
        for d in range(1, nz):
            z_copy(s, d).wait_send()

    for k in range(2):
        core_copy(k).wait_send()
    for e in hops:
        r_copy(e).wait_send()
        g_copy(e, core * chips + chip).wait_send()
    for e in range(chips):
        f_copy(e, last, core * chips + whence(e)).wait_send()
        out_copy(e, last, core * chips + whence(e)).wait()
        f_copy(e, last, (1 - core) * chips + whence(e)).wait_recv()


def finish_kernel(messages, out_hbm, held, out_v, in_sem, out_sem):
    shards = held.shape[0] // 2
    per = PAIRS // shards
    step = 8 * per

    def load(g):
        rows = pl.ds(g * step, step if g < FBD // 8 else MARK)
        return pltpu.make_async_copy(messages.at[:, rows], held.at[:, rows], in_sem.at[g])

    def store(g):
        rows = pl.ds(g * 8 * TILE, 8 * TILE)
        return pltpu.make_async_copy(out_v.at[rows], out_hbm.at[rows], out_sem.at[g])

    load(FBD // 8).start()
    for g in range(FBD // 8):
        load(g).start()
    load(FBD // 8).wait()
    scales = []
    for q in range(2 * shards):
        mark = held[q, FBD * per : FBD * per + MARK].astype(jnp.int32).astype(jnp.float32)
        scales.append(jnp.exp2(mark[:1]) * (1.0 / TOP))
    for g in range(FBD // 8):
        load(g).wait()
        for q in range(2 * shards):
            value = held[q, g * step : (g + 1) * step].astype(jnp.int32).astype(jnp.float32) * scales[q]
            for n in range(per):
                j = 2 * ((q % shards) * per + n) + q // shards
                out_v[pl.ds(g * 8 * TILE + j, 8, stride=TILE), :] = value[n * 8 : (n + 1) * 8]
        store(g).start()
    for g in range(FBD // 8):
        store(g).wait()


def local(ny, nx, nz, duals, tiles, tile_rows, tile_cols, block_counts, probabilities, customer_map, costs):
    scen = duals.shape[0]
    bf16, f32 = jnp.bfloat16, jnp.float32
    chips = ny * nx
    rows = PAIRS // chips * FBD
    i16 = jnp.int16
    hbm = pl.BlockSpec(memory_space=pltpu.HBM)
    dma = pltpu.SemaphoreType.DMA
    sems = dma((chips,))
    deep = min(DEEP, scen)
    messages = pl.pallas_call(
        functools.partial(exchange_kernel, ny, nx, nz, scen),
        out_shape=jax.ShapeDtypeStruct((2 * chips, rows + MARK, LANES), i16),
        in_specs=[hbm] * 8,
        out_specs=hbm,
        scratch_shapes=[
            pltpu.VMEM(tile_rows.shape, jnp.int32),
            pltpu.VMEM(tile_cols.shape, jnp.int32),
            pltpu.SMEM((scen,), jnp.int32),
            pltpu.SMEM((scen,), f32),
            pltpu.SMEM(customer_map.shape, jnp.int32),
            pltpu.VMEM(duals.shape, bf16),
            pltpu.VMEM(tiles.shape, bf16),
            pltpu.VMEM((scen, nz, TILE, LANES), bf16),
            pltpu.VMEM((scen, nz, TILE, LANES), bf16),
            pltpu.VMEM((nz * FBD, SLOTS), bf16),
            pltpu.VMEM((deep, PAIRS * FBD, nz * LANES), bf16),
            pltpu.VMEM((deep, PAIRS * FBD, nz * LANES), bf16),
            pltpu.VMEM((nz * LANES, 2 * LANES), bf16),
            pltpu.VMEM((TILE, FBD, LANES), f32),
            pltpu.VMEM((PAIRS, FBD, LANES), f32),
            pltpu.VMEM((PAIRS // chips, FBD, LANES), f32),
            pltpu.VMEM((chips, rows + MARK, LANES), i16),
            pltpu.VMEM((chips, rows + MARK, LANES), i16),
            pltpu.VMEM((rows + MARK, LANES), i16),
            pltpu.VMEM((2 * chips, rows + MARK, LANES), i16),
            dma((5,)),
            dma,
            dma((scen,)),
            dma((scen, nz)),
            dma((scen, nz)),
            dma((2,)),
            dma((2,)),
        ]
        + [sems] * 6
        + [dma((PAIRS // chips,)), sems],
        compiler_params=pltpu.CompilerParams(
            collective_id=0, has_side_effects=True, vmem_limit_bytes=62 * 2**20
        ),
        name="exchange",
    )(duals, tiles, tile_rows, tile_cols, block_counts.reshape(scen), probabilities, customer_map, costs.reshape(FBD, TILE, LANES))
    return pl.pallas_call(
        finish_kernel,
        out_shape=jax.ShapeDtypeStruct(costs.shape, f32),
        in_specs=[hbm],
        out_specs=hbm,
        scratch_shapes=[
            pltpu.VMEM(messages.shape, i16),
            pltpu.VMEM(costs.shape, f32),
            dma((FBD // 8 + 1,)),
            dma((FBD // 8,)),
        ],
        compiler_params=pltpu.CompilerParams(vmem_limit_bytes=62 * 2**20),
        name="finish",
    )(messages)


def solution(mesh):
    nz = mesh.shape["fac"]
    chips = mesh.shape["scen"] // 2
    side = 1
    while side * side < chips:
        side += 1
    in_specs = (
        P("scen", "fac", None),
        P("scen", "fac", None),
        P("scen", "fac"),
        P("scen", "fac"),
        P("scen", "fac"),
        P("scen"),
        P(),
        P("fac", None),
    )
    out_specs = P("fac", None)
    return jax.shard_map(
        functools.partial(local, side, side, nz),
        mesh=mesh,
        in_specs=in_specs,
        out_specs=out_specs,
        check_vma=False,
    )
```

```python
import functools

import jax
import jax.numpy as jnp
from jax import lax
from jax.experimental import pallas as pl
from jax.experimental.pallas import tpu as pltpu
from jax.sharding import PartitionSpec as P

TILE = 64
FBD = 40
SLOTS = 128
LANES = 128
PAIRS = TILE // 2
WIDE = 16
DEEP = 5
TOP = 32000.0
MARK = 16
GROUP = 5
MESH = pl.DeviceIdType.MESH


def coded(value):
    most = jnp.max(jnp.abs(value), axis=0, keepdims=True)
    power = jnp.ceil(jnp.log2(jnp.maximum(most, 1e-30)))
    steps = jnp.floor(value * (jnp.exp2(-power) * TOP) + 0.5)
    mark = jnp.broadcast_to(power, (MARK, LANES))
    return jnp.concatenate([steps, mark], axis=0).astype(jnp.int32).astype(jnp.int16)


def decoded(message):
    wide = message.astype(jnp.int32).astype(jnp.float32)
    return wide[:-MARK] * (jnp.exp2(wide[-MARK : 1 - MARK]) * (1.0 / TOP))


def by_eight(value):
    count = value.shape[0]
    return jnp.concatenate([value[m, c : c + 8] for c in range(0, FBD, 8) for m in range(count)], axis=0)


def exchange_kernel(
    ny,
    nx,
    nz,
    scen,
    duals_hbm,
    tiles_hbm,
    rows_hbm,
    cols_hbm,
    counts_hbm,
    prob_hbm,
    map_hbm,
    costs_hbm,
    out,
    rows_ref,
    cols_ref,
    counts_ref,
    prob_ref,
    map_ref,
    duals_v,
    tiles_v,
    stage,
    land,
    selector,
    dense,
    weights,
    acc,
    core_in,
    own_costs,
    r_out,
    r_in,
    last,
    gathered,
    small_sem,
    duals_sem,
    tiles_sem,
    z_send,
    z_recv,
    c_send,
    c_recv,
    r_send,
    r_recv,
    g_send,
    g_recv,
    f_send,
    f_recv,
    own_sem,
    out_sem,
):
    sc = lax.axis_index("scen")
    me = lax.axis_index("fac")
    core = lax.rem(sc, 2)
    xx = lax.rem(lax.div(sc, 2), nx)
    yy = lax.div(sc, 2 * nx)
    chips = ny * nx
    chip = lax.div(sc, 2)

    def at(y, x, c):
        return (lax.rem(y, ny) * nx + lax.rem(x, nx)) * 2 + c

    sibling = (at(yy, xx, 1 - core), me)

    barrier = pltpu.get_barrier_semaphore()
    peers = [(sc, lax.rem(me + d, nz)) for d in range(1, nz)]
    peers += [(at(yy + e // nx, xx + e % nx, core), me) for e in range(1, chips)]
    peers.append(sibling)
    for one in peers:
        pl.semaphore_signal(barrier, inc=1, device_id=one, device_id_type=MESH)

    duals_copy = pltpu.make_async_copy(duals_hbm, duals_v, duals_sem)
    pairs = ((map_hbm, map_ref), (rows_hbm, rows_ref), (cols_hbm, cols_ref), (counts_hbm, counts_ref), (prob_hbm, prob_ref))
    smalls = [pltpu.make_async_copy(src, dst, small_sem.at[n]) for n, (src, dst) in enumerate(pairs)]
    smalls[0].start()
    duals_copy.start()
    for one in smalls[1:]:
        one.start()

    per = PAIRS // chips

    def costs_copy(n):
        j = 2 * (chip * per + n) + core
        return pltpu.make_async_copy(costs_hbm.at[:, j], own_costs.at[n], own_sem.at[n])

    for n in range(per):
        costs_copy(n).start()

    def tiles_copy(s):
        return pltpu.make_async_copy(tiles_hbm.at[s], tiles_v.at[s], tiles_sem.at[s])

    @pl.loop(0, scen)
    def _(s):
        tiles_copy(s).start()

    weights[...] = jnp.zeros_like(weights)
    acc[...] = jnp.zeros_like(acc)
    for one in smalls:
        one.wait()

    owners = [map_ref[me * nz + k] for k in range(nz)]
    keep = [[jnp.where(owner == o, 1.0, 0.0) for owner in owners] for o in range(nz)]
    duals_copy.wait()

    @pl.loop(0, scen)
    def _(s):
        blocks = [duals_v[s, k * TILE : (k + 1) * TILE, :].astype(jnp.float32) for k in range(nz)]
        for o in range(nz):
            block = blocks[0] * keep[o][0]
            for k in range(1, nz):
                block = block + blocks[k] * keep[o][k]
            stage[s, o] = block.astype(jnp.bfloat16)

    def densify(s):
        slot = lax.rem(s, DEEP)
        position = lax.broadcasted_iota(jnp.int32, (1, SLOTS), 1)
        cells = rows_ref[pl.ds(s, 1), :] * FBD + cols_ref[pl.ds(s, 1), :]
        cells = jnp.where(position < counts_ref[s], cells, -1)
        cell_ids = lax.broadcasted_iota(jnp.int32, (nz * FBD, SLOTS), 0)
        selector[...] = jnp.where(cell_ids == cells, 1.0, 0.0).astype(jnp.bfloat16)
        tiles_copy(s).wait()
        for n in range(WIDE):
            block = tiles_v[s, :, n * 256 : (n + 1) * 256]
            value = jnp.dot(selector[...], block, preferred_element_type=jnp.float32)
            for r in range(nz):
                part = value[r * FBD : (r + 1) * FBD]
                both = jnp.concatenate([part[:, :LANES], part[:, LANES:]], axis=0)
                upper = both.astype(jnp.bfloat16)
                lower = (both - upper.astype(jnp.float32)).astype(jnp.bfloat16)
                dense[slot, n * 80 : (n + 1) * 80, r * LANES : (r + 1) * LANES] = upper
                dense[slot, n * 80 : (n + 1) * 80, (nz + r) * LANES : (nz + r + 1) * LANES] = lower

    pl.semaphore_wait(barrier, len(peers))

    def z_copy(s, d):
        to = lax.rem(me + d, nz)
        return pltpu.make_async_remote_copy(
            src_ref=stage.at[s, to],
            dst_ref=land.at[s, me],
            send_sem=z_send.at[s, d],
            recv_sem=z_recv.at[s, d],
            device_id=(sc, to),
            device_id_type=MESH,
        )

    def z_arrival(s, d):
        source = lax.rem(me + nz - d, nz)
        return pltpu.make_async_remote_copy(
            src_ref=stage.at[s, source],
            dst_ref=land.at[s, source],
            send_sem=z_send.at[s, d],
            recv_sem=z_recv.at[s, d],
            device_id=(sc, source),
            device_id_type=MESH,
        )

    order = sorted(range(1, nz), key=lambda d: -min(d, nz - d))

    @pl.loop(0, scen)
    def _(s):
        for d in order:
            z_copy(s, d).start()
        land[s, me] = stage[s, me]

    @pl.loop(0, min(DEEP, scen))
    def _(s):
        densify(s)

    mine = core * PAIRS
    other = (1 - core) * PAIRS

    @pl.loop(0, scen)
    def _(s):
        slot = lax.rem(s, DEEP)
        for d in range(1, nz):
            z_arrival(s, d).wait_recv()
        for r in range(nz):
            block = land[s, r]
            for n in (r, nz + r):
                weights[n * LANES : n * LANES + TILE, :LANES] = block
                weights[n * LANES + TILE : (n + 1) * LANES, LANES:] = block

        scale = prob_ref[s]
        value = jnp.dot(dense[slot], weights[...], preferred_element_type=jnp.float32)
        value = value * scale
        acc[:PAIRS] += value[:, :LANES].reshape(PAIRS, FBD, LANES)
        acc[PAIRS:] += value[:, LANES:].reshape(PAIRS, FBD, LANES)

        @pl.when(s < scen - DEEP)
        def _():
            densify(s + DEEP)

    def remote(src, dst, send, recv, to):
        return pltpu.make_async_remote_copy(
            src_ref=src, dst_ref=dst, send_sem=send, recv_sem=recv, device_id=to, device_id_type=MESH
        )

    def there(e):
        return lax.rem(yy + e // nx, ny) * nx + lax.rem(xx + e % nx, nx)

    def whence(e):
        return lax.rem(yy + ny - e // nx, ny) * nx + lax.rem(xx + nx - e % nx, nx)

    def r_copy(e):
        to = there(e)
        return remote(r_out.at[to], r_in.at[e], r_send.at[e], r_recv.at[e], (to * 2 + core, me))

    def g_copy(e, shard):
        return remote(last, gathered.at[shard], g_send.at[e], g_recv.at[e], (there(e) * 2 + core, me))

    def f_copy(e, src, shard):
        return remote(src, out.at[shard], f_send.at[e], f_recv.at[e], sibling)

    def out_copy(e, src, shard):
        return pltpu.make_async_copy(src, out.at[shard], out_sem.at[e])

    hops = sorted(range(1, chips), key=lambda e: -min(e // nx, ny - e // nx) - min(e % nx, nx - e % nx))
    core_copy = remote(acc.at[pl.ds(other, PAIRS)], core_in, c_send, c_recv, sibling)
    core_copy.start()
    core_copy.wait_recv()
    for first in range(0, chips - 1, GROUP):
        group = hops[first : first + GROUP]
        values = [acc[pl.ds(mine + there(e) * per, per)] + core_in[pl.ds(there(e) * per, per)] for e in group]
        messages = [coded(by_eight(value)) for value in values]
        for e, message in zip(group, messages):
            r_out[there(e)] = message
        for e in group:
            r_copy(e).start()
    total = acc[pl.ds(mine + chip * per, per)] + core_in[pl.ds(chip * per, per)]
    for n in range(per):
        costs_copy(n).wait()
    total = by_eight(own_costs[...] - total)
    for e in hops:
        r_copy(e).wait_recv()
        total = total - decoded(r_in[e])
    shard = core * chips + chip
    last[...] = coded(total)
    for e in hops:
        g_copy(e, shard).start()
    f_copy(0, last, shard).start()
    out_copy(0, last, shard).start()
    for e in reversed(hops):
        shard = core * chips + whence(e)
        g_copy(e, shard).wait_recv()
        f_copy(e, gathered.at[shard], shard).start()
        out_copy(e, gathered.at[shard], shard).start()

    @pl.loop(0, scen)
    def _(s):
        for d in range(1, nz):
            z_copy(s, d).wait_send()

    core_copy.wait_send()
    for e in hops:
        r_copy(e).wait_send()
        g_copy(e, core * chips + chip).wait_send()
    for e in range(chips):
        f_copy(e, last, core * chips + whence(e)).wait_send()
        out_copy(e, last, core * chips + whence(e)).wait()
        f_copy(e, last, (1 - core) * chips + whence(e)).wait_recv()


def finish_kernel(messages, out_hbm, held, out_v, in_sem, out_sem):
    shards = held.shape[0] // 2
    per = PAIRS // shards
    step = 8 * per

    def load(g):
        rows = pl.ds(g * step, step if g < FBD // 8 else MARK)
        return pltpu.make_async_copy(messages.at[:, rows], held.at[:, rows], in_sem.at[g])

    def store(g):
        rows = pl.ds(g * 8 * TILE, 8 * TILE)
        return pltpu.make_async_copy(out_v.at[rows], out_hbm.at[rows], out_sem.at[g])

    load(FBD // 8).start()
    for g in range(FBD // 8):
        load(g).start()
    load(FBD // 8).wait()
    scales = []
    for q in range(2 * shards):
        mark = held[q, FBD * per : FBD * per + MARK].astype(jnp.int32).astype(jnp.float32)
        scales.append(jnp.exp2(mark[:1]) * (1.0 / TOP))
    for g in range(FBD // 8):
        load(g).wait()
        for q in range(2 * shards):
            value = held[q, g * step : (g + 1) * step].astype(jnp.int32).astype(jnp.float32) * scales[q]
            for n in range(per):
                j = 2 * ((q % shards) * per + n) + q // shards
                out_v[pl.ds(g * 8 * TILE + j, 8, stride=TILE), :] = value[n * 8 : (n + 1) * 8]
        store(g).start()
    for g in range(FBD // 8):
        store(g).wait()


def local(ny, nx, nz, duals, tiles, tile_rows, tile_cols, block_counts, probabilities, customer_map, costs):
    scen = duals.shape[0]
    bf16, f32 = jnp.bfloat16, jnp.float32
    chips = ny * nx
    rows = PAIRS // chips * FBD
    i16 = jnp.int16
    hbm = pl.BlockSpec(memory_space=pltpu.HBM)
    dma = pltpu.SemaphoreType.DMA
    sems = dma((chips,))
    deep = min(DEEP, scen)
    messages = pl.pallas_call(
        functools.partial(exchange_kernel, ny, nx, nz, scen),
        out_shape=jax.ShapeDtypeStruct((2 * chips, rows + MARK, LANES), i16),
        in_specs=[hbm] * 8,
        out_specs=hbm,
        scratch_shapes=[
            pltpu.VMEM(tile_rows.shape, jnp.int32),
            pltpu.VMEM(tile_cols.shape, jnp.int32),
            pltpu.SMEM((scen,), jnp.int32),
            pltpu.SMEM((scen,), f32),
            pltpu.SMEM(customer_map.shape, jnp.int32),
            pltpu.VMEM(duals.shape, bf16),
            pltpu.VMEM(tiles.shape, bf16),
            pltpu.VMEM((scen, nz, TILE, LANES), bf16),
            pltpu.VMEM((scen, nz, TILE, LANES), bf16),
            pltpu.VMEM((nz * FBD, SLOTS), bf16),
            pltpu.VMEM((deep, PAIRS * FBD, 2 * nz * LANES), bf16),
            pltpu.VMEM((2 * nz * LANES, 2 * LANES), bf16),
            pltpu.VMEM((TILE, FBD, LANES), f32),
            pltpu.VMEM((PAIRS, FBD, LANES), f32),
            pltpu.VMEM((PAIRS // chips, FBD, LANES), f32),
            pltpu.VMEM((chips, rows + MARK, LANES), i16),
            pltpu.VMEM((chips, rows + MARK, LANES), i16),
            pltpu.VMEM((rows + MARK, LANES), i16),
            pltpu.VMEM((2 * chips, rows + MARK, LANES), i16),
            dma((5,)),
            dma,
            dma((scen,)),
            dma((scen, nz)),
            dma((scen, nz)),
            dma,
            dma,
        ]
        + [sems] * 6
        + [dma((PAIRS // chips,)), sems],
        compiler_params=pltpu.CompilerParams(
            collective_id=0, has_side_effects=True, vmem_limit_bytes=62 * 2**20
        ),
        name="exchange",
    )(duals, tiles, tile_rows, tile_cols, block_counts.reshape(scen), probabilities, customer_map, costs.reshape(FBD, TILE, LANES))
    return pl.pallas_call(
        finish_kernel,
        out_shape=jax.ShapeDtypeStruct(costs.shape, f32),
        in_specs=[hbm],
        out_specs=hbm,
        scratch_shapes=[
            pltpu.VMEM(messages.shape, i16),
            pltpu.VMEM(costs.shape, f32),
            dma((FBD // 8 + 1,)),
            dma((FBD // 8,)),
        ],
        compiler_params=pltpu.CompilerParams(vmem_limit_bytes=62 * 2**20),
        name="finish",
    )(messages)


def solution(mesh):
    nz = mesh.shape["fac"]
    chips = mesh.shape["scen"] // 2
    side = 1
    while side * side < chips:
        side += 1
    in_specs = (
        P("scen", "fac", None),
        P("scen", "fac", None),
        P("scen", "fac"),
        P("scen", "fac"),
        P("scen", "fac"),
        P("scen"),
        P(),
        P("fac", None),
    )
    out_specs = P("fac", None)
    return jax.shard_map(
        functools.partial(local, side, side, nz),
        mesh=mesh,
        in_specs=in_specs,
        out_specs=out_specs,
        check_vma=False,
    )
```

```python
import functools

import jax
import jax.numpy as jnp
from jax import lax
from jax.experimental import pallas as pl
from jax.experimental.pallas import tpu as pltpu
from jax.sharding import PartitionSpec as P

TILE = 64
FBD = 40
SLOTS = 128
LANES = 128
PAIRS = TILE // 2
WIDE = 16
DEEP = 5
TOP = 32000.0
MARK = 16
GROUP = 5
MESH = pl.DeviceIdType.MESH


def coded(value):
    most = jnp.max(jnp.abs(value), axis=0, keepdims=True)
    power = jnp.ceil(jnp.log2(jnp.maximum(most, 1e-30)))
    steps = jnp.floor(value * (jnp.exp2(-power) * TOP) + 0.5)
    mark = jnp.broadcast_to(power, (MARK, LANES))
    return jnp.concatenate([steps, mark], axis=0).astype(jnp.int32).astype(jnp.int16)


def decoded(message):
    wide = message.astype(jnp.int32).astype(jnp.float32)
    return wide[:-MARK] * (jnp.exp2(wide[-MARK : 1 - MARK]) * (1.0 / TOP))


def by_eight(value):
    count = value.shape[0]
    return jnp.concatenate([value[m, c : c + 8] for c in range(0, FBD, 8) for m in range(count)], axis=0)


def exchange_kernel(
    ny,
    nx,
    nz,
    scen,
    duals_hbm,
    tiles_hbm,
    rows_hbm,
    cols_hbm,
    counts_hbm,
    prob_hbm,
    map_hbm,
    costs_hbm,
    out,
    rows_ref,
    cols_ref,
    counts_ref,
    prob_ref,
    map_ref,
    duals_v,
    tiles_v,
    stage,
    land,
    selector,
    dense,
    weights,
    acc,
    core_in,
    own_costs,
    r_out,
    r_in,
    last,
    gathered,
    small_sem,
    duals_sem,
    tiles_sem,
    z_send,
    z_recv,
    c_send,
    c_recv,
    r_send,
    r_recv,
    g_send,
    g_recv,
    f_send,
    f_recv,
    own_sem,
    out_sem,
):
    sc = lax.axis_index("scen")
    me = lax.axis_index("fac")
    core = lax.rem(sc, 2)
    xx = lax.rem(lax.div(sc, 2), nx)
    yy = lax.div(sc, 2 * nx)
    chips = ny * nx
    chip = lax.div(sc, 2)

    def at(y, x, c):
        return (lax.rem(y, ny) * nx + lax.rem(x, nx)) * 2 + c

    sibling = (at(yy, xx, 1 - core), me)

    barrier = pltpu.get_barrier_semaphore()
    peers = [(sc, lax.rem(me + d, nz)) for d in range(1, nz)]
    peers += [(at(yy + e // nx, xx + e % nx, core), me) for e in range(1, chips)]
    peers.append(sibling)
    for one in peers:
        pl.semaphore_signal(barrier, inc=1, device_id=one, device_id_type=MESH)

    duals_copy = pltpu.make_async_copy(duals_hbm, duals_v, duals_sem)
    pairs = ((map_hbm, map_ref), (rows_hbm, rows_ref), (cols_hbm, cols_ref), (counts_hbm, counts_ref), (prob_hbm, prob_ref))
    smalls = [pltpu.make_async_copy(src, dst, small_sem.at[n]) for n, (src, dst) in enumerate(pairs)]
    smalls[0].start()
    duals_copy.start()
    for one in smalls[1:]:
        one.start()

    per = PAIRS // chips

    def costs_copy(n):
        j = 2 * (chip * per + n) + core
        return pltpu.make_async_copy(costs_hbm.at[:, j], own_costs.at[n], own_sem.at[n])

    for n in range(per):
        costs_copy(n).start()

    def tiles_copy(s):
        return pltpu.make_async_copy(tiles_hbm.at[s], tiles_v.at[s], tiles_sem.at[s])

    @pl.loop(0, scen)
    def _(s):
        tiles_copy(s).start()

    weights[...] = jnp.zeros_like(weights)
    acc[...] = jnp.zeros_like(acc)
    for one in smalls:
        one.wait()

    owners = [map_ref[me * nz + k] for k in range(nz)]
    keep = [[jnp.where(owner == o, 1.0, 0.0) for owner in owners] for o in range(nz)]
    duals_copy.wait()

    @pl.loop(0, scen)
    def _(s):
        blocks = [duals_v[s, k * TILE : (k + 1) * TILE, :].astype(jnp.float32) for k in range(nz)]
        for o in range(nz):
            block = blocks[0] * keep[o][0]
            for k in range(1, nz):
                block = block + blocks[k] * keep[o][k]
            stage[s, o] = block.astype(jnp.bfloat16)

    def densify(s):
        slot = lax.rem(s, DEEP)
        position = lax.broadcasted_iota(jnp.int32, (1, SLOTS), 1)
        cells = rows_ref[pl.ds(s, 1), :] * FBD + cols_ref[pl.ds(s, 1), :]
        cells = jnp.where(position < counts_ref[s], cells, -1)
        cell_ids = lax.broadcasted_iota(jnp.int32, (nz * FBD, SLOTS), 0)
        selector[...] = jnp.where(cell_ids == cells, 1.0, 0.0).astype(jnp.bfloat16)
        tiles_copy(s).wait()
        for n in range(WIDE):
            block = tiles_v[s, :, n * 256 : (n + 1) * 256]
            value = jnp.dot(selector[...], block, preferred_element_type=jnp.float32)
            for r in range(nz):
                part = value[r * FBD : (r + 1) * FBD]
                both = jnp.concatenate([part[:, :LANES], part[:, LANES:]], axis=0)
                upper = both.astype(jnp.bfloat16)
                lower = (both - upper.astype(jnp.float32)).astype(jnp.bfloat16)
                dense[slot, n * 80 : (n + 1) * 80, r * LANES : (r + 1) * LANES] = upper
                dense[slot, n * 80 : (n + 1) * 80, (nz + r) * LANES : (nz + r + 1) * LANES] = lower

    pl.semaphore_wait(barrier, len(peers))

    def z_copy(s, d):
        to = lax.rem(me + d, nz)
        return pltpu.make_async_remote_copy(
            src_ref=stage.at[s, to],
            dst_ref=land.at[s, me],
            send_sem=z_send.at[s, d],
            recv_sem=z_recv.at[s, d],
            device_id=(sc, to),
            device_id_type=MESH,
        )

    def z_arrival(s, d):
        source = lax.rem(me + nz - d, nz)
        return pltpu.make_async_remote_copy(
            src_ref=stage.at[s, source],
            dst_ref=land.at[s, source],
            send_sem=z_send.at[s, d],
            recv_sem=z_recv.at[s, d],
            device_id=(sc, source),
            device_id_type=MESH,
        )

    order = sorted(range(1, nz), key=lambda d: -min(d, nz - d))

    @pl.loop(0, scen)
    def _(s):
        for d in order:
            z_copy(s, d).start()
        land[s, me] = stage[s, me]

    @pl.loop(0, min(DEEP, scen))
    def _(s):
        densify(s)

    mine = core * PAIRS
    other = (1 - core) * PAIRS

    part = PAIRS // 2

    def core_copy(k):
        return pltpu.make_async_remote_copy(
            src_ref=acc.at[pl.ds(other + k * part, part)],
            dst_ref=core_in.at[pl.ds(k * part, part)],
            send_sem=c_send.at[k],
            recv_sem=c_recv.at[k],
            device_id=sibling,
            device_id_type=MESH,
        )

    def gather_weights(s):
        for d in range(1, nz):
            z_arrival(s, d).wait_recv()
        for r in range(nz):
            block = land[s, r]
            for n in (r, nz + r):
                weights[n * LANES : n * LANES + TILE, :LANES] = block
                weights[n * LANES + TILE : (n + 1) * LANES, LANES:] = block

    def multiply(s, start, count):
        rows = slice(start * FBD, (start + count) * FBD)
        value = jnp.dot(dense[s % DEEP if isinstance(s, int) else lax.rem(s, DEEP), rows], weights[...], preferred_element_type=jnp.float32)
        value = value * prob_ref[s]
        acc[start : start + count] += value[:, :LANES].reshape(count, FBD, LANES)
        acc[PAIRS + start : PAIRS + start + count] += value[:, LANES:].reshape(count, FBD, LANES)

    @pl.loop(0, scen - 1)
    def _(s):
        gather_weights(s)
        multiply(s, 0, PAIRS)

        @pl.when(s < scen - DEEP)
        def _():
            densify(s + DEEP)

    final = scen - 1
    gather_weights(final)
    for k in range(2):
        multiply(final, k * part, part // 2)
        multiply(final, k * part + part // 2, part // 2)
        core_copy(k).start()

    def remote(src, dst, send, recv, to):
        return pltpu.make_async_remote_copy(
            src_ref=src, dst_ref=dst, send_sem=send, recv_sem=recv, device_id=to, device_id_type=MESH
        )

    def there(e):
        return lax.rem(yy + e // nx, ny) * nx + lax.rem(xx + e % nx, nx)

    def whence(e):
        return lax.rem(yy + ny - e // nx, ny) * nx + lax.rem(xx + nx - e % nx, nx)

    def r_copy(e):
        to = there(e)
        return remote(r_out.at[to], r_in.at[e], r_send.at[e], r_recv.at[e], (to * 2 + core, me))

    def g_copy(e, shard):
        return remote(last, gathered.at[shard], g_send.at[e], g_recv.at[e], (there(e) * 2 + core, me))

    def f_copy(e, src, shard):
        return remote(src, out.at[shard], f_send.at[e], f_recv.at[e], sibling)

    def out_copy(e, src, shard):
        return pltpu.make_async_copy(src, out.at[shard], out_sem.at[e])

    hops = sorted(range(1, chips), key=lambda e: -min(e // nx, ny - e // nx) - min(e % nx, nx - e % nx))
    for k in range(2):
        core_copy(k).wait_recv()
    for first in range(0, chips - 1, GROUP):
        group = hops[first : first + GROUP]
        values = [acc[pl.ds(mine + there(e) * per, per)] + core_in[pl.ds(there(e) * per, per)] for e in group]
        messages = [coded(by_eight(value)) for value in values]
        for e, message in zip(group, messages):
            r_out[there(e)] = message
        for e in group:
            r_copy(e).start()
    total = acc[pl.ds(mine + chip * per, per)] + core_in[pl.ds(chip * per, per)]
    for n in range(per):
        costs_copy(n).wait()
    total = by_eight(own_costs[...] - total)
    for e in hops:
        r_copy(e).wait_recv()
        total = total - decoded(r_in[e])
    shard = core * chips + chip
    last[...] = coded(total)
    for e in hops:
        g_copy(e, shard).start()
    f_copy(0, last, shard).start()
    out_copy(0, last, shard).start()
    for e in reversed(hops):
        shard = core * chips + whence(e)
        g_copy(e, shard).wait_recv()
        f_copy(e, gathered.at[shard], shard).start()
        out_copy(e, gathered.at[shard], shard).start()

    @pl.loop(0, scen)
    def _(s):
        for d in range(1, nz):
            z_copy(s, d).wait_send()

    for k in range(2):
        core_copy(k).wait_send()
    for e in hops:
        r_copy(e).wait_send()
        g_copy(e, core * chips + chip).wait_send()
    for e in range(chips):
        f_copy(e, last, core * chips + whence(e)).wait_send()
        out_copy(e, last, core * chips + whence(e)).wait()
        f_copy(e, last, (1 - core) * chips + whence(e)).wait_recv()


def finish_kernel(messages, out_hbm, held, out_v, in_sem, out_sem):
    shards = held.shape[0] // 2
    per = PAIRS // shards
    step = 8 * per

    def load(g):
        rows = pl.ds(g * step, step if g < FBD // 8 else MARK)
        return pltpu.make_async_copy(messages.at[:, rows], held.at[:, rows], in_sem.at[g])

    def store(g):
        rows = pl.ds(g * 8 * TILE, 8 * TILE)
        return pltpu.make_async_copy(out_v.at[rows], out_hbm.at[rows], out_sem.at[g])

    load(FBD // 8).start()
    for g in range(FBD // 8):
        load(g).start()
    load(FBD // 8).wait()
    scales = []
    for q in range(2 * shards):
        mark = held[q, FBD * per : FBD * per + MARK].astype(jnp.int32).astype(jnp.float32)
        scales.append(jnp.exp2(mark[:1]) * (1.0 / TOP))
    for g in range(FBD // 8):
        load(g).wait()
        for q in range(2 * shards):
            value = held[q, g * step : (g + 1) * step].astype(jnp.int32).astype(jnp.float32) * scales[q]
            for n in range(per):
                j = 2 * ((q % shards) * per + n) + q // shards
                out_v[pl.ds(g * 8 * TILE + j, 8, stride=TILE), :] = value[n * 8 : (n + 1) * 8]
        store(g).start()
    for g in range(FBD // 8):
        store(g).wait()


def local(ny, nx, nz, duals, tiles, tile_rows, tile_cols, block_counts, probabilities, customer_map, costs):
    scen = duals.shape[0]
    bf16, f32 = jnp.bfloat16, jnp.float32
    chips = ny * nx
    rows = PAIRS // chips * FBD
    i16 = jnp.int16
    hbm = pl.BlockSpec(memory_space=pltpu.HBM)
    dma = pltpu.SemaphoreType.DMA
    sems = dma((chips,))
    deep = min(DEEP, scen)
    messages = pl.pallas_call(
        functools.partial(exchange_kernel, ny, nx, nz, scen),
        out_shape=jax.ShapeDtypeStruct((2 * chips, rows + MARK, LANES), i16),
        in_specs=[hbm] * 8,
        out_specs=hbm,
        scratch_shapes=[
            pltpu.VMEM(tile_rows.shape, jnp.int32),
            pltpu.VMEM(tile_cols.shape, jnp.int32),
            pltpu.SMEM((scen,), jnp.int32),
            pltpu.SMEM((scen,), f32),
            pltpu.SMEM(customer_map.shape, jnp.int32),
            pltpu.VMEM(duals.shape, bf16),
            pltpu.VMEM(tiles.shape, bf16),
            pltpu.VMEM((scen, nz, TILE, LANES), bf16),
            pltpu.VMEM((scen, nz, TILE, LANES), bf16),
            pltpu.VMEM((nz * FBD, SLOTS), bf16),
            pltpu.VMEM((deep, PAIRS * FBD, 2 * nz * LANES), bf16),
            pltpu.VMEM((2 * nz * LANES, 2 * LANES), bf16),
            pltpu.VMEM((TILE, FBD, LANES), f32),
            pltpu.VMEM((PAIRS, FBD, LANES), f32),
            pltpu.VMEM((PAIRS // chips, FBD, LANES), f32),
            pltpu.VMEM((chips, rows + MARK, LANES), i16),
            pltpu.VMEM((chips, rows + MARK, LANES), i16),
            pltpu.VMEM((rows + MARK, LANES), i16),
            pltpu.VMEM((2 * chips, rows + MARK, LANES), i16),
            dma((5,)),
            dma,
            dma((scen,)),
            dma((scen, nz)),
            dma((scen, nz)),
            dma((2,)),
            dma((2,)),
        ]
        + [sems] * 6
        + [dma((PAIRS // chips,)), sems],
        compiler_params=pltpu.CompilerParams(
            collective_id=0, has_side_effects=True, vmem_limit_bytes=62 * 2**20
        ),
        name="exchange",
    )(duals, tiles, tile_rows, tile_cols, block_counts.reshape(scen), probabilities, customer_map, costs.reshape(FBD, TILE, LANES))
    return pl.pallas_call(
        finish_kernel,
        out_shape=jax.ShapeDtypeStruct(costs.shape, f32),
        in_specs=[hbm],
        out_specs=hbm,
        scratch_shapes=[
            pltpu.VMEM(messages.shape, i16),
            pltpu.VMEM(costs.shape, f32),
            dma((FBD // 8 + 1,)),
            dma((FBD // 8,)),
        ],
        compiler_params=pltpu.CompilerParams(vmem_limit_bytes=62 * 2**20),
        name="finish",
    )(messages)


def solution(mesh):
    nz = mesh.shape["fac"]
    chips = mesh.shape["scen"] // 2
    side = 1
    while side * side < chips:
        side += 1
    in_specs = (
        P("scen", "fac", None),
        P("scen", "fac", None),
        P("scen", "fac"),
        P("scen", "fac"),
        P("scen", "fac"),
        P("scen"),
        P(),
        P("fac", None),
    )
    out_specs = P("fac", None)
    return jax.shard_map(
        functools.partial(local, side, side, nz),
        mesh=mesh,
        in_specs=in_specs,
        out_specs=out_specs,
        check_vma=False,
    )
```

```python
import functools

import jax
import jax.numpy as jnp
from jax import lax
from jax.experimental import pallas as pl
from jax.experimental.pallas import tpu as pltpu
from jax.sharding import PartitionSpec as P

TILE = 64
FBD = 40
SLOTS = 128
LANES = 128
PAIRS = TILE // 2
WIDE = 16
DEEP = 5
TOP = 32000.0
MARK = 16
GROUP = 5
MESH = pl.DeviceIdType.MESH


def coded(value):
    most = jnp.max(jnp.abs(value), axis=0, keepdims=True)
    power = jnp.ceil(jnp.log2(jnp.maximum(most, 1e-30)))
    steps = jnp.floor(value * (jnp.exp2(-power) * TOP) + 0.5)
    mark = jnp.broadcast_to(power, (MARK, LANES))
    return jnp.concatenate([steps, mark], axis=0).astype(jnp.int32).astype(jnp.int16)


def decoded(message):
    wide = message.astype(jnp.int32).astype(jnp.float32)
    return wide[:-MARK] * (jnp.exp2(wide[-MARK : 1 - MARK]) * (1.0 / TOP))


def by_eight(value):
    count = value.shape[0]
    return jnp.concatenate([value[m, c : c + 8] for c in range(0, FBD, 8) for m in range(count)], axis=0)


def exchange_kernel(
    ny,
    nx,
    nz,
    scen,
    duals_hbm,
    tiles_hbm,
    rows_hbm,
    cols_hbm,
    counts_hbm,
    prob_hbm,
    map_hbm,
    costs_hbm,
    out,
    rows_ref,
    cols_ref,
    counts_ref,
    prob_ref,
    map_ref,
    duals_v,
    tiles_v,
    stage,
    land,
    selector,
    dense,
    weights,
    acc,
    core_in,
    own_costs,
    r_out,
    r_in,
    last,
    gathered,
    small_sem,
    duals_sem,
    tiles_sem,
    z_send,
    z_recv,
    c_send,
    c_recv,
    r_send,
    r_recv,
    g_send,
    g_recv,
    f_send,
    f_recv,
    own_sem,
    out_sem,
):
    sc = lax.axis_index("scen")
    me = lax.axis_index("fac")
    core = lax.rem(sc, 2)
    xx = lax.rem(lax.div(sc, 2), nx)
    yy = lax.div(sc, 2 * nx)
    chips = ny * nx
    chip = lax.div(sc, 2)

    def at(y, x, c):
        return (lax.rem(y, ny) * nx + lax.rem(x, nx)) * 2 + c

    sibling = (at(yy, xx, 1 - core), me)

    barrier = pltpu.get_barrier_semaphore()
    peers = [(sc, lax.rem(me + d, nz)) for d in range(1, nz)]
    peers += [(at(yy + e // nx, xx + e % nx, core), me) for e in range(1, chips)]
    peers.append(sibling)
    for one in peers:
        pl.semaphore_signal(barrier, inc=1, device_id=one, device_id_type=MESH)

    duals_copy = pltpu.make_async_copy(duals_hbm, duals_v, duals_sem)
    pairs = ((map_hbm, map_ref), (rows_hbm, rows_ref), (cols_hbm, cols_ref), (counts_hbm, counts_ref), (prob_hbm, prob_ref))
    smalls = [pltpu.make_async_copy(src, dst, small_sem.at[n]) for n, (src, dst) in enumerate(pairs)]
    smalls[0].start()
    duals_copy.start()
    for one in smalls[1:]:
        one.start()

    per = PAIRS // chips

    def costs_copy(n):
        j = 2 * (chip * per + n) + core
        return pltpu.make_async_copy(costs_hbm.at[:, j], own_costs.at[n], own_sem.at[n])

    for n in range(per):
        costs_copy(n).start()

    def tiles_copy(s):
        return pltpu.make_async_copy(tiles_hbm.at[s], tiles_v.at[s], tiles_sem.at[s])

    @pl.loop(0, scen)
    def _(s):
        tiles_copy(s).start()

    weights[...] = jnp.zeros_like(weights)
    acc[...] = jnp.zeros_like(acc)
    for one in smalls:
        one.wait()

    owners = [map_ref[me * nz + k] for k in range(nz)]
    keep = [[jnp.where(owner == o, 1.0, 0.0) for owner in owners] for o in range(nz)]
    duals_copy.wait()

    @pl.loop(0, scen)
    def _(s):
        blocks = [duals_v[s, k * TILE : (k + 1) * TILE, :].astype(jnp.float32) for k in range(nz)]
        for o in range(nz):
            block = blocks[0] * keep[o][0]
            for k in range(1, nz):
                block = block + blocks[k] * keep[o][k]
            stage[s, o] = block.astype(jnp.bfloat16)

    def densify(s):
        slot = lax.rem(s, DEEP)
        position = lax.broadcasted_iota(jnp.int32, (1, SLOTS), 1)
        cells = rows_ref[pl.ds(s, 1), :] * FBD + cols_ref[pl.ds(s, 1), :]
        cells = jnp.where(position < counts_ref[s], cells, -1)
        cell_ids = lax.broadcasted_iota(jnp.int32, (nz * FBD, SLOTS), 0)
        selector[...] = jnp.where(cell_ids == cells, 1.0, 0.0).astype(jnp.bfloat16)
        tiles_copy(s).wait()
        for n in range(WIDE):
            block = tiles_v[s, :, n * 256 : (n + 1) * 256]
            value = jnp.dot(selector[...], block, preferred_element_type=jnp.float32)
            for r in range(nz):
                part = value[r * FBD : (r + 1) * FBD]
                both = jnp.concatenate([part[:, :LANES], part[:, LANES:]], axis=0)
                upper = both.astype(jnp.bfloat16)
                lower = (both - upper.astype(jnp.float32)).astype(jnp.bfloat16)
                dense[slot, n * 80 : (n + 1) * 80, r * LANES : (r + 1) * LANES] = upper
                dense[slot, n * 80 : (n + 1) * 80, (nz + r) * LANES : (nz + r + 1) * LANES] = lower

    pl.semaphore_wait(barrier, len(peers))

    def z_copy(s, d):
        to = lax.rem(me + d, nz)
        return pltpu.make_async_remote_copy(
            src_ref=stage.at[s, to],
            dst_ref=land.at[s, me],
            send_sem=z_send.at[s, d],
            recv_sem=z_recv.at[s, d],
            device_id=(sc, to),
            device_id_type=MESH,
        )

    def z_arrival(s, d):
        source = lax.rem(me + nz - d, nz)
        return pltpu.make_async_remote_copy(
            src_ref=stage.at[s, source],
            dst_ref=land.at[s, source],
            send_sem=z_send.at[s, d],
            recv_sem=z_recv.at[s, d],
            device_id=(sc, source),
            device_id_type=MESH,
        )

    order = sorted(range(1, nz), key=lambda d: -min(d, nz - d))

    @pl.loop(0, scen)
    def _(s):
        for d in order:
            z_copy(s, d).start()
        land[s, me] = stage[s, me]

    @pl.loop(0, min(DEEP, scen))
    def _(s):
        densify(s)

    mine = core * PAIRS
    other = (1 - core) * PAIRS

    part = PAIRS // 2

    def core_copy(k):
        return pltpu.make_async_remote_copy(
            src_ref=acc.at[pl.ds(other + k * part, part)],
            dst_ref=core_in.at[pl.ds(k * part, part)],
            send_sem=c_send.at[k],
            recv_sem=c_recv.at[k],
            device_id=sibling,
            device_id_type=MESH,
        )

    def gather_weights(s):
        for d in range(1, nz):
            z_arrival(s, d).wait_recv()
        for r in range(nz):
            block = land[s, r]
            for n in (r, nz + r):
                weights[n * LANES : n * LANES + TILE, :LANES] = block
                weights[n * LANES + TILE : (n + 1) * LANES, LANES:] = block

    def multiply(s, start, count):
        rows = slice(start * FBD, (start + count) * FBD)
        value = jnp.dot(dense[s % DEEP if isinstance(s, int) else lax.rem(s, DEEP), rows], weights[...], preferred_element_type=jnp.float32)
        value = value * prob_ref[s]
        acc[start : start + count] += value[:, :LANES].reshape(count, FBD, LANES)
        acc[PAIRS + start : PAIRS + start + count] += value[:, LANES:].reshape(count, FBD, LANES)

    @pl.loop(0, scen - 1)
    def _(s):
        gather_weights(s)
        multiply(s, 0, PAIRS)

        @pl.when(s < scen - DEEP)
        def _():
            densify(s + DEEP)

    final = scen - 1
    gather_weights(final)
    for k in range(2):
        multiply(final, k * part, part // 2)
        multiply(final, k * part + part // 2, part // 2)
        core_copy(k).start()

    def remote(src, dst, send, recv, to):
        return pltpu.make_async_remote_copy(
            src_ref=src, dst_ref=dst, send_sem=send, recv_sem=recv, device_id=to, device_id_type=MESH
        )

    def there(e):
        return lax.rem(yy + e // nx, ny) * nx + lax.rem(xx + e % nx, nx)

    def whence(e):
        return lax.rem(yy + ny - e // nx, ny) * nx + lax.rem(xx + nx - e % nx, nx)

    def r_copy(e):
        to = there(e)
        return remote(r_out.at[to], r_in.at[e], r_send.at[e], r_recv.at[e], (to * 2 + core, me))

    def g_copy(e, shard):
        return remote(last, gathered.at[shard], g_send.at[e], g_recv.at[e], (there(e) * 2 + core, me))

    def f_copy(e, src, shard):
        return remote(src, out.at[shard], f_send.at[e], f_recv.at[e], sibling)

    def out_copy(e, src, shard):
        return pltpu.make_async_copy(src, out.at[shard], out_sem.at[e])

    hops = sorted(range(1, chips), key=lambda e: -min(e // nx, ny - e // nx) - min(e % nx, nx - e % nx))
    for k in range(2):
        core_copy(k).wait_recv()
    for first in range(0, chips - 1, GROUP):
        group = hops[first : first + GROUP]
        values = [acc[pl.ds(mine + there(e) * per, per)] + core_in[pl.ds(there(e) * per, per)] for e in group]
        messages = [coded(by_eight(value)) for value in values]
        for e, message in zip(group, messages):
            r_out[there(e)] = message
        for e in group:
            r_copy(e).start()
    total = acc[pl.ds(mine + chip * per, per)] + core_in[pl.ds(chip * per, per)]
    for n in range(per):
        costs_copy(n).wait()
    total = by_eight(own_costs[...] - total)
    for e in hops:
        r_copy(e).wait_recv()
        total = total - decoded(r_in[e])
    shard = core * chips + chip
    last[...] = coded(total)
    for e in hops:
        g_copy(e, shard).start()
    f_copy(0, last, shard).start()
    out_copy(0, last, shard).start()
    for e in reversed(hops):
        shard = core * chips + whence(e)
        g_copy(e, shard).wait_recv()
        f_copy(e, gathered.at[shard], shard).start()
        out_copy(e, gathered.at[shard], shard).start()

    @pl.loop(0, scen)
    def _(s):
        for d in range(1, nz):
            z_copy(s, d).wait_send()

    for k in range(2):
        core_copy(k).wait_send()
    for e in hops:
        r_copy(e).wait_send()
        g_copy(e, core * chips + chip).wait_send()
    for e in range(chips):
        f_copy(e, last, core * chips + whence(e)).wait_send()
        out_copy(e, last, core * chips + whence(e)).wait()
        f_copy(e, last, (1 - core) * chips + whence(e)).wait_recv()


def finish_kernel(messages, out_hbm, held, out_v, in_sem, out_sem):
    shards = held.shape[0] // 2
    per = PAIRS // shards
    step = 8 * per

    def load(g):
        rows = pl.ds(g * step, step if g < FBD // 8 else MARK)
        return pltpu.make_async_copy(messages.at[:, rows], held.at[:, rows], in_sem.at[g])

    def store(g):
        rows = pl.ds(g * 8 * TILE, 8 * TILE)
        return pltpu.make_async_copy(out_v.at[rows], out_hbm.at[rows], out_sem.at[g])

    load(FBD // 8).start()
    for g in range(FBD // 8):
        load(g).start()
    load(FBD // 8).wait()
    scales = []
    for q in range(2 * shards):
        mark = held[q, FBD * per : FBD * per + MARK].astype(jnp.int32).astype(jnp.float32)
        scales.append(jnp.exp2(mark[:1]) * (1.0 / TOP))
    for g in range(FBD // 8):
        load(g).wait()
        for q in range(2 * shards):
            value = held[q, g * step : (g + 1) * step].astype(jnp.int32).astype(jnp.float32) * scales[q]
            for n in range(per):
                j = 2 * ((q % shards) * per + n) + q // shards
                out_v[pl.ds(g * 8 * TILE + j, 8, stride=TILE), :] = value[n * 8 : (n + 1) * 8]
        store(g).start()
    for g in range(FBD // 8):
        store(g).wait()


def local(ny, nx, nz, duals, tiles, tile_rows, tile_cols, block_counts, probabilities, customer_map, costs):
    scen = duals.shape[0]
    bf16, f32 = jnp.bfloat16, jnp.float32
    chips = ny * nx
    rows = PAIRS // chips * FBD
    i16 = jnp.int16
    hbm = pl.BlockSpec(memory_space=pltpu.HBM)
    dma = pltpu.SemaphoreType.DMA
    sems = dma((chips,))
    deep = min(DEEP, scen)
    messages = pl.pallas_call(
        functools.partial(exchange_kernel, ny, nx, nz, scen),
        out_shape=jax.ShapeDtypeStruct((2 * chips, rows + MARK, LANES), i16),
        in_specs=[hbm] * 8,
        out_specs=hbm,
        scratch_shapes=[
            pltpu.VMEM(tile_rows.shape, jnp.int32),
            pltpu.VMEM(tile_cols.shape, jnp.int32),
            pltpu.SMEM((scen,), jnp.int32),
            pltpu.SMEM((scen,), f32),
            pltpu.SMEM(customer_map.shape, jnp.int32),
            pltpu.VMEM(duals.shape, bf16),
            pltpu.VMEM(tiles.shape, bf16),
            pltpu.VMEM((scen, nz, TILE, LANES), bf16),
            pltpu.VMEM((scen, nz, TILE, LANES), bf16),
            pltpu.VMEM((nz * FBD, SLOTS), bf16),
            pltpu.VMEM((deep, PAIRS * FBD, 2 * nz * LANES), bf16),
            pltpu.VMEM((2 * nz * LANES, 2 * LANES), bf16),
            pltpu.VMEM((TILE, FBD, LANES), f32),
            pltpu.VMEM((PAIRS, FBD, LANES), f32),
            pltpu.VMEM((PAIRS // chips, FBD, LANES), f32),
            pltpu.VMEM((chips, rows + MARK, LANES), i16),
            pltpu.VMEM((chips, rows + MARK, LANES), i16),
            pltpu.VMEM((rows + MARK, LANES), i16),
            pltpu.VMEM((2 * chips, rows + MARK, LANES), i16),
            dma((5,)),
            dma,
            dma((scen,)),
            dma((scen, nz)),
            dma((scen, nz)),
            dma((2,)),
            dma((2,)),
        ]
        + [sems] * 6
        + [dma((PAIRS // chips,)), sems],
        compiler_params=pltpu.CompilerParams(
            collective_id=0, has_side_effects=True, vmem_limit_bytes=62 * 2**20
        ),
        name="exchange",
    )(duals, tiles, tile_rows, tile_cols, block_counts.reshape(scen), probabilities, customer_map, costs.reshape(FBD, TILE, LANES))
    return pl.pallas_call(
        finish_kernel,
        out_shape=jax.ShapeDtypeStruct(costs.shape, f32),
        in_specs=[hbm],
        out_specs=hbm,
        scratch_shapes=[
            pltpu.VMEM(messages.shape, i16),
            pltpu.VMEM((costs.shape[0] + TILE, LANES), f32),
            dma((FBD // 8 + 1,)),
            dma((FBD // 8,)),
        ],
        compiler_params=pltpu.CompilerParams(vmem_limit_bytes=62 * 2**20),
        name="finish",
    )(messages)


def solution(mesh):
    nz = mesh.shape["fac"]
    chips = mesh.shape["scen"] // 2
    side = 1
    while side * side < chips:
        side += 1
    in_specs = (
        P("scen", "fac", None),
        P("scen", "fac", None),
        P("scen", "fac"),
        P("scen", "fac"),
        P("scen", "fac"),
        P("scen"),
        P(),
        P("fac", None),
    )
    out_specs = P("fac", None)
    return jax.shard_map(
        functools.partial(local, side, side, nz),
        mesh=mesh,
        in_specs=in_specs,
        out_specs=out_specs,
        check_vma=False,
    )
```
